256 devices in a mesh: gx: 16 (over x_lo, y, core), gy: 8 (over z), gz: 2 (over x_hi).
Axes of the slice: x: 4 (x_hi: 2, x_lo: 2; x = x_hi * 2 + x_lo), y: 4, z: 8, core: 2. Of those that a mesh axis runs over, the one named last changes fastest.
Arguments:
- sections: bfloat16 [12, 1024, 2048], P('gz', 'gy', 'gx'), may hold values from -12 to 12
Outputs:
- corr_maps: bfloat16 [12, 2, 32, 64, 4096], P('gz', None, 'gy', 'gx')
The draws below stay inside these ranges and needn't reach their ends.
All inputs are finite; a program needn't handle non-finite values.
Results may differ from the reference program's by a relative error of at most 0.011.
Values may be sent and summed in bfloat16 or wider, within the bound.
No kernel may reach another device: no remote copies, remote signals or barrier semaphores. Data moves between devices by JAX's collectives and lax.ppermute only.
A program may use at most 64 MiB of HBM per device.

```python
import math
import jax
import jax.numpy as jnp
from jax import lax

PATCH = 64
STRIDE = 32
SECT = 12
NROW = 1024
NCOL = 2048


def draw_sections(key, part):
    key = jax.random.fold_in(key, 7)
    key_common = jax.random.fold_in(key, 1)
    key_smooth = jax.random.fold_in(key, 2)
    key_noise = jax.random.fold_in(key, 3)
    key_mixing = jax.random.fold_in(key, 4)
    common = jax.random.truncated_normal(key_common, -3.5, 3.5, (1, NROW, NCOL), jnp.float32)
    source = jax.random.truncated_normal(key_smooth, -3.5, 3.5, (1, NROW, NCOL), jnp.float32)
    noise = jax.random.truncated_normal(key_noise, -3.5, 3.5, (SECT, NROW, NCOL), jnp.float32)
    blurred = jnp.zeros_like(source)
    for step_row in (-1, 0, 1):
        for step_col in (-1, 0, 1):
            blurred = blurred + jnp.roll(source, (step_row, step_col), (1, 2))
    texture = (common + blurred * (2.0 / 9.0)) * (1.0 / 1.2)
    mixing = jax.random.uniform(key_mixing, (SECT, 1, 1), jnp.float32, 0.4, 0.9)
    return (mixing * texture + jnp.sqrt(1.0 - mixing * mixing) * noise).astype(jnp.bfloat16)


def setup_inputs(seed: int = 0) -> dict:
    key_list = jax.random.split(jax.random.key(seed), 2)
    sections = draw_sections(jax.random.fold_in(key_list[1], 71), 0)
    return dict(sections=sections)


def tables():
    indices = jnp.arange(PATCH, dtype=jnp.int32)
    product = indices[:, None] * indices[None, :] % PATCH
    angles = product.astype(jnp.float32) * (2.0 * math.pi / PATCH)
    cosine = jnp.cos(angles).astype(jnp.bfloat16)
    sine_table = jnp.sin(angles).astype(jnp.bfloat16)
    first_table = jnp.concatenate([cosine, -sine_table], 1)
    inverse = jnp.concatenate([jnp.concatenate([cosine, sine_table], 1), jnp.concatenate([-sine_table, cosine], 1)], 0)
    last_table = jnp.stack([cosine, -sine_table], 2)
    return (first_table, cosine, sine_table, inverse, last_table)

def cut_patches(padded):
    count, rows, cols = padded.shape
    n_rows = rows // STRIDE - 1
    n_cols = cols // STRIDE - 1
    blocks = padded.reshape(count, n_rows + 1, STRIDE, cols)
    row_pairs = jnp.concatenate([blocks[:, :-1], blocks[:, 1:]], axis=2)
    col_blocks = row_pairs.reshape(count, n_rows, PATCH, n_cols + 1, STRIDE)
    both = jnp.concatenate([col_blocks[:, :, :, :-1], col_blocks[:, :, :, 1:]], axis=4)
    return both.transpose(0, 1, 3, 2, 4)

def forward(pixels, first_table, cosine, sine_table):
    pixels = pixels.astype(jnp.float32)
    centre = lax.optimization_barrier(jnp.mean(pixels, axis=(-2, -1), keepdims=True))
    centered = pixels - centre
    spread = lax.optimization_barrier(jnp.mean(centered * centered, axis=(-2, -1), keepdims=True))
    normed = (centered * lax.rsqrt(spread + 1e-05) * (1.0 / PATCH)).astype(jnp.bfloat16)
    g_cat = jnp.einsum('...xy,yc->...xc', normed.astype(jnp.float32), first_table.astype(jnp.float32)).astype(jnp.bfloat16)
    along_cos = jnp.einsum('ux,...xc->...uc', cosine.astype(jnp.float32), g_cat.astype(jnp.float32))
    along_sin = jnp.einsum('ux,...xc->...uc', sine_table.astype(jnp.float32), g_cat.astype(jnp.float32))
    f_re = along_cos[..., :PATCH] + along_sin[..., PATCH:]
    f_im = along_cos[..., PATCH:] - along_sin[..., :PATCH]
    return jnp.concatenate([f_re, f_im], -1).astype(jnp.bfloat16)

def correlate(spec_here, spec_next, inverse, last_table):
    here = spec_here.astype(jnp.float32)
    there = spec_next.astype(jnp.float32)
    q_re = here[..., :PATCH] * there[..., :PATCH] + here[..., PATCH:] * there[..., PATCH:]
    q_im = here[..., PATCH:] * there[..., :PATCH] - here[..., :PATCH] * there[..., PATCH:]
    q_cat = jnp.concatenate([q_re, q_im], -1).astype(jnp.bfloat16)
    h_cat = jnp.einsum('...uc,cd->...ud', q_cat.astype(jnp.float32), inverse.astype(jnp.float32)).astype(jnp.bfloat16)
    h_split = h_cat.reshape(h_cat.shape[:-1] + (2, PATCH))
    maps = jnp.einsum('xuk,...uky->...xy', last_table.astype(jnp.float32), h_split.astype(jnp.float32))
    maps = maps * (1.0 / (PATCH * PATCH))
    return maps.reshape(maps.shape[:-2] + (PATCH * PATCH,)).astype(jnp.bfloat16)

def reference(sections):
    first_table, cosine, sine_table, inverse, last_table = tables()
    half = STRIDE // 2
    padded = jnp.pad(sections, ((0, 0), (half, half), (half, half)))

    def section_spectra(single):
        return forward(cut_patches(single[None])[0], first_table, cosine, sine_table)
    spectra = lax.map(section_spectra, padded)

    def pair_maps(index):
        results = []
        for lag in (1, 2):
            target = jnp.minimum(index + lag, SECT - 1).astype(jnp.int32)
            inside = index + lag < SECT
            partner = jnp.where(inside, spectra[target], jnp.zeros_like(spectra[0]))
            results.append(correlate(spectra[index], partner, inverse, last_table))
        return jnp.stack(results, 0)
    return lax.map(pair_maps, jnp.arange(SECT, dtype=jnp.int32))
```

```python
import functools
import math

import jax
import jax.numpy as jnp
import ml_dtypes
import numpy as np
from jax import lax
from jax.experimental import pallas as pl
from jax.experimental.pallas import tpu as pltpu
from jax.sharding import PartitionSpec as P

PATCH = 64
F32 = jnp.float32
BF16 = jnp.bfloat16
VMEM = pl.BlockSpec(memory_space=pltpu.VMEM)
ANY = pl.BlockSpec(memory_space=pl.ANY)


def rounded(values):
    return values.astype(np.float32).astype(ml_dtypes.bfloat16)


@functools.cache
def constants():
    index = np.arange(PATCH)
    angle = (index[:, None] * index[None, :] % PATCH) * (2.0 * math.pi / PATCH)
    cos = rounded(np.cos(angle)).astype(np.float64)
    sin = rounded(np.sin(angle)).astype(np.float64)
    sign = 1.0 - 2.0 * (index % 2)

    rows = np.zeros((160, 2, 4, 32))
    for j in range(4):
        rows[32 * j : 32 * j + 64, 0, j] = cos[:, :32]
        rows[32 * j : 32 * j + 64, 1, j] = -sin[:, :32]
        rows[32 * j : 32 * j + 64, 1, j, 0] = sign
    rows = rows.reshape(160, 256)

    forward = np.block([[cos, sin], [-sin, cos]])
    order = np.concatenate([index[0::2], index[1::2]])
    inverse = np.block([[cos[order], -sin[order]], [sin[order], cos[order]]])

    last = np.zeros((2, 4, 32, 4, 64))
    weight = np.where(index[:32] == 0, 1.0, 2.0)[:, None] / 4096.0
    for j in range(4):
        last[0, j, :, j] = weight * cos[:32]
        last[1, j, :, j] = -weight * sin[:32]
        last[1, j, 0, j] = sign / 4096.0
    even = last.reshape(256, 256)
    odd = last[:, :, :, [1, 0, 3, 2]].reshape(256, 256)

    column = np.full(256, -1000)
    column[:128] = np.arange(128) + 16
    column[128:144] = np.arange(16)
    column[192:208] = np.arange(16) + 144
    inside = np.stack([(column >= 32 * j) & (column < 32 * j + 64) for j in range(4)], 1)
    inside = inside.astype(np.float64)
    same_even = inside[:, [0, 2]] @ inside[:, [0, 2]].T
    same_odd = inside[:, [1, 3]] @ inside[:, [1, 3]].T
    spread = np.repeat(inside, 32, axis=1)
    lane_odd = (np.arange(128) // 32 % 2).astype(np.float64)
    means = np.concatenate([same_even, same_odd, spread], 1)
    totals = np.concatenate([spread * (1 - lane_odd), spread * lane_odd], 0)
    return dict(
        own=rounded(rows[16:144]),
        sides=rounded(np.concatenate([rows[:16], rows[144:]], 0)),
        forward=rounded(forward),
        inverse=rounded(inverse),
        even=rounded(even),
        odd=rounded(odd),
        means=rounded(means),
        totals=rounded(totals),
    )


NAMES = ("own", "sides", "forward", "inverse", "even", "odd", "means", "totals")


def dot(a, b):
    return jnp.dot(a, b, preferred_element_type=F32)


def dot_exact(a, ones):
    high = a.astype(BF16)
    rest = a - high.astype(F32)
    middle = rest.astype(BF16)
    low = (rest - middle.astype(F32)).astype(BF16)
    n = a.shape[0]
    parts = dot(jnp.concatenate([high, middle, low], 0), ones)
    return parts[2 * n :] + parts[n : 2 * n] + parts[:n]


def lanes(shape):
    return lax.broadcasted_iota(jnp.int32, shape, len(shape) - 1)


def edges_kernel(s_ref, a_ref, b_ref):
    odd = lax.axis_index("gx") % 2 == 1
    lane = lanes((128, 128))
    left = jnp.zeros((128, 128), F32)
    right = jnp.zeros((128, 128), F32)
    for s in range(6):
        block = s_ref[s].astype(F32)
        here = (lane // 16) == s
        first = pltpu.roll(block, 16 * s, 1) if s else block
        last = pltpu.roll(block, 16 * s + 16, 1)
        left = jnp.where(here, first, left)
        right = jnp.where(here, last, right)
    left = left.astype(BF16)
    right = right.astype(BF16)
    a_ref[...] = jnp.where(odd, left, right)
    b_ref[...] = jnp.where(odd, right, left)


def rows_kernel(s_ref, xa_ref, xb_ref, e_ref, a_ref, b_ref, z_ref):
    odd_x = lax.axis_index("gx") % 2 == 1
    odd_y = lax.axis_index("gy") % 2 == 1
    xa = xa_ref[...].astype(F32)
    xb = xb_ref[...].astype(F32)
    left = jnp.where(odd_x, xa, xb)
    right = jnp.where(odd_x, xb, xa)
    low = lanes((128, 128)) < 64
    e0 = jnp.where(low, left, pltpu.roll(right, 64, 1)).astype(BF16)
    e1 = jnp.where(low, pltpu.roll(left, 64, 1), right).astype(BF16)
    e_ref[0] = e0
    e_ref[1] = e1
    first = jnp.concatenate([s_ref[s, :16] for s in range(6)] + [e0[:16], e1[:16]], 0)
    last = jnp.concatenate([s_ref[s, 112:] for s in range(6)] + [e0[112:], e1[112:]], 0)
    a_ref[...] = jnp.where(odd_y, first, last)
    b_ref[...] = jnp.where(odd_y, last, first)
    z_ref[0] = s_ref[0]
    z_ref[1] = s_ref[1]
    z_ref[2] = e0


def spectra(count, first, slot_f, own, edge, ya_ref, yb_ref, flag, c, w):
    odd_y = lax.axis_index("gy") % 2 == 1
    top = jnp.where(odd_y, ya_ref[...], yb_ref[...])
    bottom = jnp.where(odd_y, yb_ref[...], ya_ref[...])
    lane = lanes((64, 128))
    zero_slot = lane % 32 == 0
    row_lane = lanes((8, 128))
    sides = c["sides"][...]
    groups = []
    for g in range((count + 3) // 4):
        groups.append(
            jnp.concatenate(
                [top[96 + 16 * g : 112 + 16 * g], edge(g), bottom[96 + 16 * g : 112 + 16 * g]], 0
            )
        )

    def column_stats(block):
        block = block.astype(F32).reshape(5, 32, 128)
        mean = jnp.sum(block, 1, keepdims=True) * (1.0 / 32)
        centred = block - mean
        return mean[:, 0], jnp.sum(centred * centred, 1)

    edge_stats = [column_stats(g) for g in groups]
    w["mu"][...] = jnp.zeros(w["mu"].shape, F32)
    w["sq"][...] = jnp.zeros(w["sq"].shape, F32)
    for s in range(count):
        q, g = s % 4, s // 4
        block = jnp.concatenate([top[16 * s : 16 * s + 16], own(s), bottom[16 * s : 16 * s + 16]], 0)
        gap0 = jnp.zeros((16 * q, 256), BF16)
        gap1 = jnp.zeros((48 - 16 * q, 256), BF16)
        pieces = [c["own"][...], gap0, sides[:16], gap1, gap0, sides[16:], gap1]
        table = jnp.concatenate([p for p in pieces if p.shape[0]], 0)
        w["g"][s] = dot(jnp.concatenate([block, groups[g]], 1), table)
        mean, square = column_stats(block)
        mean_e, square_e = edge_stats[g]
        if q:
            mean_e = pltpu.roll(mean_e, 128 - 16 * q, 1)
            square_e = pltpu.roll(square_e, 128 - 16 * q, 1)
        w["mu"][:, s, :128] = mean
        w["mu"][:, s, 128:] = mean_e
        w["sq"][:, s, :128] = square
        w["sq"][:, s, 128:] = square_e

    mu = w["mu"][...]
    sq = w["sq"][...]
    mu0, mu1 = mu[:4].reshape(32, 256), mu[1:].reshape(32, 256)
    sq01 = (sq[:4] + sq[1:]).reshape(32, 256)
    sums = dot_exact(mu0 + mu1, c["means"][...])
    total = []
    for parity in range(2):
        centre = sums[:, 256 * parity : 256 * parity + 256] * (1.0 / 128)
        d0, d1 = mu0 - centre, mu1 - centre
        total.append(sq01 + 32.0 * (d0 * d0 + d1 * d1))
    variance = dot_exact(jnp.concatenate(total, 1), c["totals"][...]) * (1.0 / 4096)
    scale = lax.rsqrt(variance + 1e-05) * (1.0 / PATCH)
    if flag is not None:
        scale = scale * flag
    w["scale"][...] = scale.reshape(4, 8, 128)
    centre = jnp.where(lanes((32, 128)) % 32 == 0, sums[:, 512:] * 0.5, 0.0)
    w["centre"][...] = centre.reshape(4, 8, 128)

    w["g32"][...] = jnp.zeros(w["g32"].shape, F32)

    def section(s, carry):
        for pair in range(2):
            columns = []
            for i in (2 * pair, 2 * pair + 1):
                re = w["g"][s, 32 * i : 32 * i + 64, :128] - w["centre"][i, pl.ds(s, 1), :]
                im = w["g"][s, 32 * i : 32 * i + 64, 128:]
                slot = 4 * (s + first) + i
                w["g32"][...] = jnp.where(lane % 32 == slot, pltpu.roll(im, slot, 1), w["g32"][...])
                im = jnp.where(zero_slot, 0.0, im)
                columns.append(jnp.concatenate([re, im], 0).astype(BF16))
            f = dot(c["forward"][...], jnp.concatenate(columns, 1))
            for n, i in enumerate((2 * pair, 2 * pair + 1)):
                part = f[:, 128 * n : 128 * n + 128] * w["scale"][i, pl.ds(s, 1), :]
                w["f"][s + slot_f, i] = part.astype(BF16)
        return carry

    lax.fori_loop(0, count, section, 0)

    scale32 = jnp.zeros((8, 128), F32)
    sublane = lax.broadcasted_iota(jnp.int32, (8, 128), 0)
    for i in range(4):
        scale32 = scale32 + jnp.where(row_lane % 32 == 4 * (sublane + first) + i, w["scale"][i], 0.0)
    scale32 = jnp.sum(scale32, 0, keepdims=True)
    f = dot(c["forward"][:, :64], w["g32"][...].astype(BF16))
    return (f * scale32).astype(BF16)


def maps(lo, hi, f32, offset, c, w, o_ref):
    f32 = f32.astype(F32)
    re, im = f32[:64], f32[64:]
    for k in range(2):
        re_p = pltpu.roll(re, 128 - 4 * (k + 1), 1)
        im_p = pltpu.roll(im, 128 - 4 * (k + 1), 1)
        q = jnp.concatenate([re * re_p + im * im_p, im * re_p - re * im_p], 0).astype(BF16)
        w["h32"][k] = dot(c["inverse"][:64], q)
    lane = lanes((64, 128))
    zero_slot = lane % 32 == 0
    low = lanes((32, 128)) < 64

    def copy(p):
        return pltpu.make_async_copy(
            w["o"].at[p - lo], o_ref.at[p // 2, p % 2], w["sem"].at[p - lo]
        )

    def pair(p, carry):
        s, k = p // 2, p % 2
        even, odd = [], []
        for half in range(2):
            columns = []
            for i in (2 * half, 2 * half + 1):
                here = w["f"][s - offset, i].astype(F32)
                there = w["f"][s + k + 1 - offset, i].astype(F32)
                f_re, f_im, p_re, p_im = here[:64], here[64:], there[:64], there[64:]
                q = jnp.concatenate([f_re * p_re + f_im * p_im, f_im * p_re - f_re * p_im], 0)
                columns.append(q.astype(BF16))
            h = dot(c["inverse"][...], jnp.concatenate(columns, 1))
            for n, i in enumerate((2 * half, 2 * half + 1)):
                h_re = h[:64, 128 * n : 128 * n + 128]
                special = pltpu.roll(w["h32"][k], 128 - (4 * s + i), 1)
                h_im = jnp.where(zero_slot, special, h[64:, 128 * n : 128 * n + 128])
                h_cat = jnp.concatenate([h_re, h_im], 1).astype(BF16)
                even.append(h_cat[:32])
                odd.append(h_cat[32:])
        even = dot(jnp.concatenate(even, 0), c["even"][...])
        odd = dot(jnp.concatenate(odd, 0), c["odd"][...])
        for i in range(4):
            for half in range(2):
                e = even[32 * i : 32 * i + 32, 128 * half : 128 * half + 128]
                o = odd[32 * i : 32 * i + 32, 128 * half : 128 * half + 128]
                w["mix"][i, pl.ds(2 * half, 32, stride=4), :] = jnp.where(low, e, o)
                w["mix"][i, pl.ds(2 * half + 1, 32, stride=4), :] = pltpu.roll(
                    jnp.where(low, o, e), 64, 1
                )
            w["o"][p - lo, i] = w["mix"][i].astype(BF16)
        copy(p).start()
        return carry

    lax.fori_loop(lo, hi, pair, 0)
    for p in range(lo, hi):
        copy(p).wait()


SCRATCH = dict(
    g=lambda n: pltpu.VMEM((n, 160, 256), F32),
    mu=lambda n: pltpu.VMEM((5, 8, 256), F32),
    sq=lambda n: pltpu.VMEM((5, 8, 256), F32),
    scale=lambda n: pltpu.VMEM((4, 8, 128), F32),
    centre=lambda n: pltpu.VMEM((4, 8, 128), F32),
    g32=lambda n: pltpu.VMEM((64, 128), F32),
    h32=lambda n: pltpu.VMEM((2, 64, 128), F32),
    mix=lambda n: pltpu.VMEM((4, 128, 128), F32),
)


def own_kernel(s_ref, e_ref, ya_ref, yb_ref, *refs):
    c = dict(zip(NAMES, refs[: len(NAMES)]))
    o_ref, f_ref, f32_ref = refs[len(NAMES) : len(NAMES) + 3]
    w = dict(zip((*SCRATCH, "o", "sem"), refs[len(NAMES) + 3 :]))
    w["f"] = f_ref
    f32 = spectra(6, 0, 0, lambda s: s_ref[s], lambda g: e_ref[g], ya_ref, yb_ref, None, c, w)
    f32_ref[...] = f32
    maps(0, 9, f32, 0, c, w, o_ref)


def rest_kernel(z_ref, ya_ref, yb_ref, f_ref, f32_ref, *refs):
    c = dict(zip(NAMES, refs[: len(NAMES)]))
    o_ref = refs[len(NAMES) + 1]
    w = dict(zip((*SCRATCH, "f", "o", "sem"), refs[len(NAMES) + 2 :]))
    flag = jnp.where(lax.axis_index("gz") == 0, 1.0, 0.0)
    w["f"][0] = f_ref[4]
    w["f"][1] = f_ref[5]
    extra = spectra(2, 6, 2, lambda s: z_ref[s], lambda g: z_ref[2], ya_ref, yb_ref, flag, c, w)
    f32 = jnp.where(lanes((128, 128)) % 32 >= 24, extra.astype(F32), f32_ref[...].astype(F32))
    maps(9, 12, f32, 4, c, w, o_ref)


def exchange(value_a, value_b, axis, count):
    pairs_a = [(n, n ^ 1) for n in range(count)]
    pairs_b = [(n, n + 1 if n % 2 else n - 1) for n in range(1, count - 1)]
    return lax.ppermute(value_a, axis, pairs_a), lax.ppermute(value_b, axis, pairs_b)


def other(value):
    return lax.ppermute(value, "gz", [(0, 1), (1, 0)])


def shaped(*shape):
    return jax.ShapeDtypeStruct(shape, BF16)


def local(sections):
    table = [jnp.asarray(constants()[name]) for name in NAMES]
    params = pltpu.CompilerParams(vmem_limit_bytes=32 * 2**20)
    edge = shaped(128, 128)
    xa, xb = pl.pallas_call(
        edges_kernel, out_shape=(edge, edge), in_specs=[VMEM], out_specs=(VMEM, VMEM)
    )(sections)
    xa, xb = exchange(xa, xb, "gx", lax.axis_size("gx"))
    edges, ya, yb, z = pl.pallas_call(
        rows_kernel,
        out_shape=(shaped(2, 128, 128), edge, edge, shaped(3, 128, 128)),
        in_specs=[VMEM] * 3,
        out_specs=(VMEM,) * 4,
    )(sections, xa, xb)
    ya, yb = exchange(ya, yb, "gy", lax.axis_size("gy"))
    z = other(z)
    za, zb = other(ya), other(yb)
    scratch = [make(6) for make in SCRATCH.values()]
    out, f, f32 = pl.pallas_call(
        own_kernel,
        out_shape=(shaped(6, 2, 4, 128, 128), shaped(6, 4, 128, 128), edge),
        in_specs=[VMEM] * (4 + len(table)),
        out_specs=(ANY, VMEM, VMEM),
        scratch_shapes=scratch + [pltpu.VMEM((9, 4, 128, 128), BF16), pltpu.SemaphoreType.DMA((9,))],
        compiler_params=params,
        cost_estimate=pl.CostEstimate(flops=10**9, bytes_accessed=4 * 10**6, transcendentals=0),
    )(sections, edges, ya, yb, *table)
    scratch = [make(2) for make in SCRATCH.values()]
    out = pl.pallas_call(
        rest_kernel,
        out_shape=shaped(6, 2, 4, 128, 128),
        in_specs=[VMEM] * (5 + len(table)) + [ANY],
        out_specs=ANY,
        scratch_shapes=scratch
        + [
            pltpu.VMEM((4, 4, 128, 128), BF16),
            pltpu.VMEM((3, 4, 128, 128), BF16),
            pltpu.SemaphoreType.DMA((3,)),
        ],
        input_output_aliases={5 + len(table): 0},
        compiler_params=params,
    )(z, za, zb, f, f32, *table, out)
    out = out.reshape(6, 2, 4, 32, 4, 128).transpose(0, 1, 2, 4, 3, 5)
    return out.reshape(6, 2, 4, 4, 4096)


def solution(mesh):
    return jax.shard_map(
        local,
        mesh=mesh,
        in_specs=(P("gz", "gy", "gx"),),
        out_specs=P("gz", None, "gy", "gx", None),
        check_vma=False,
    )
```

```python
import functools
import math

import jax
import jax.numpy as jnp
import ml_dtypes
import numpy as np
from jax import lax
from jax.experimental import pallas as pl
from jax.experimental.pallas import tpu as pltpu
from jax.sharding import PartitionSpec as P

PATCH = 64
F32 = jnp.float32
BF16 = jnp.bfloat16
VMEM = pl.BlockSpec(memory_space=pltpu.VMEM)
HBM = pl.BlockSpec(memory_space=pltpu.HBM)


def rounded(values):
    return values.astype(np.float32).astype(ml_dtypes.bfloat16)


@functools.cache
def constants():
    index = np.arange(PATCH)
    angle = (index[:, None] * index[None, :] % PATCH) * (2.0 * math.pi / PATCH)
    cos = rounded(np.cos(angle)).astype(np.float64)
    sin = rounded(np.sin(angle)).astype(np.float64)
    sign = 1.0 - 2.0 * (index % 2)

    rows = np.zeros((160, 2, 4, 32))
    for j in range(4):
        rows[32 * j : 32 * j + 64, 0, j] = cos[:, :32]
        rows[32 * j : 32 * j + 64, 1, j] = -sin[:, :32]
        rows[32 * j : 32 * j + 64, 1, j, 0] = sign
    rows = rows.reshape(160, 256)

    forward = np.block([[cos, sin], [-sin, cos]])
    order = np.concatenate([index[0::2], index[1::2]])
    inverse = np.block([[cos[order], -sin[order]], [sin[order], cos[order]]])

    last = np.zeros((2, 4, 32, 4, 64))
    weight = np.where(index[:32] == 0, 1.0, 2.0)[:, None] / 4096.0
    for j in range(4):
        last[0, j, :, j] = weight * cos[:32]
        last[1, j, :, j] = -weight * sin[:32]
        last[1, j, 0, j] = sign / 4096.0
    even = last.reshape(256, 256)
    odd = last[:, :, :, [1, 0, 3, 2]].reshape(256, 256)

    column = np.full(256, -1000)
    column[:128] = np.arange(128) + 16
    column[128:144] = np.arange(16)
    column[192:208] = np.arange(16) + 144
    inside = np.stack([(column >= 32 * j) & (column < 32 * j + 64) for j in range(4)], 1)
    inside = inside.astype(np.float64)
    same_even = inside[:, [0, 2]] @ inside[:, [0, 2]].T
    same_odd = inside[:, [1, 3]] @ inside[:, [1, 3]].T
    spread = np.repeat(inside, 32, axis=1)
    lane_odd = (np.arange(128) // 32 % 2).astype(np.float64)
    means = np.concatenate([same_even, same_odd, spread], 1)
    totals = np.concatenate([spread * (1 - lane_odd), spread * lane_odd], 0)
    tables = dict(
        own=rows[16:144],
        sides=np.concatenate([rows[:16], rows[144:]], 0),
        forward=forward,
        inverse=inverse,
        even=even,
        odd=odd,
        means=means,
        totals=totals,
    )
    pieces, places, at = [], {}, 0
    for name, table in tables.items():
        height, width = table.shape
        places[name] = (at, height, width // 128)
        pieces += np.split(table, width // 128, 1)
        at += height * width // 128
    return rounded(np.concatenate(pieces, 0)), places


class Tables:
    def __init__(self, ref):
        self.ref = ref

    def __getitem__(self, name):
        at, height, width = constants()[1][name]
        pieces = [self.ref[at + height * n : at + height * (n + 1)] for n in range(width)]
        return jnp.concatenate(pieces, 1) if width > 1 else pieces[0]


def dot(a, b):
    return jnp.dot(a, b, preferred_element_type=F32)


def dot_exact(a, ones):
    high = a.astype(BF16)
    rest = a - high.astype(F32)
    middle = rest.astype(BF16)
    low = (rest - middle.astype(F32)).astype(BF16)
    n = a.shape[0]
    parts = dot(jnp.concatenate([high, middle, low], 0), ones)
    return parts[2 * n :] + parts[n : 2 * n] + parts[:n]


def lanes(shape):
    return lax.broadcasted_iota(jnp.int32, shape, len(shape) - 1)


def edges_kernel(s_hbm, t_hbm, a_ref, b_ref, s_ref, t_ref, sem):
    sections = pltpu.make_async_copy(s_hbm, s_ref, sem.at[0])
    tables = pltpu.make_async_copy(t_hbm, t_ref, sem.at[1])
    sections.start()
    tables.start()
    sections.wait()
    odd = lax.axis_index("gx") % 2 == 1
    lane = lanes((128, 128))
    left = jnp.zeros((128, 128), F32)
    right = jnp.zeros((128, 128), F32)
    for s in range(6):
        block = s_ref[s].astype(F32)
        here = (lane // 16) == s
        first = pltpu.roll(block, 16 * s, 1) if s else block
        last = pltpu.roll(block, 16 * s + 16, 1)
        left = jnp.where(here, first, left)
        right = jnp.where(here, last, right)
    a_ref[...] = jnp.where(odd, left, right).astype(BF16)
    b_ref[...] = jnp.where(odd, right, left).astype(BF16)
    tables.wait()


def rows_kernel(s_ref, xa_ref, xb_ref, e_ref, a_ref, b_ref, z_ref):
    odd_x = lax.axis_index("gx") % 2 == 1
    odd_y = lax.axis_index("gy") % 2 == 1
    xa = xa_ref[...].astype(F32)
    xb = xb_ref[...].astype(F32)
    left = jnp.where(odd_x, xa, xb)
    right = jnp.where(odd_x, xb, xa)
    low = lanes((128, 128)) < 64
    e0 = jnp.where(low, left, pltpu.roll(right, 64, 1)).astype(BF16)
    e1 = jnp.where(low, pltpu.roll(left, 64, 1), right).astype(BF16)
    e_ref[0] = e0
    e_ref[1] = e1
    first = jnp.concatenate([s_ref[s, :16] for s in range(6)] + [e0[:16], e1[:16]], 0)
    last = jnp.concatenate([s_ref[s, 112:] for s in range(6)] + [e0[112:], e1[112:]], 0)
    a_ref[...] = jnp.where(odd_y, first, last)
    b_ref[...] = jnp.where(odd_y, last, first)
    z_ref[0] = s_ref[0]
    z_ref[1] = s_ref[1]
    z_ref[2] = e0


def halo_kernel(ya_ref, yb_ref, z_ref):
    top, bottom = halo(ya_ref, yb_ref)
    for n, at in enumerate((0, 16, 96)):
        z_ref[16 * n : 16 * n + 16] = top[at : at + 16]
        z_ref[48 + 16 * n : 64 + 16 * n] = bottom[at : at + 16]


def halo(ya_ref, yb_ref):
    odd = lax.axis_index("gy") % 2 == 1
    ya, yb = ya_ref[...], yb_ref[...]
    return jnp.where(odd, ya, yb), jnp.where(odd, yb, ya)


def spectra(count, first, slot_f, sections, edges, flag, c, w):
    lane = lanes((64, 128))
    zero_slot = lane % 32 == 0
    row_lane = lanes((8, 128))
    sides = c["sides"]
    def column_stats(block):
        block = block.astype(F32).reshape(5, 32, 128)
        mean = jnp.sum(block, 1, keepdims=True) * (1.0 / 32)
        centred = block - mean
        return mean[:, 0], jnp.sum(centred * centred, 1)

    edge_stats = [column_stats(g) for g in edges]
    w["mu"][...] = jnp.zeros(w["mu"].shape, F32)
    w["sq"][...] = jnp.zeros(w["sq"].shape, F32)
    for s in range(count):
        q, g = s % 4, s // 4
        block = sections[s]
        gap0 = jnp.zeros((16 * q, 256), BF16)
        gap1 = jnp.zeros((48 - 16 * q, 256), BF16)
        pieces = [c["own"], gap0, sides[:16], gap1, gap0, sides[16:], gap1]
        table = jnp.concatenate([p for p in pieces if p.shape[0]], 0)
        w["g"][s] = dot(jnp.concatenate([block, edges[g]], 1), table)
        mean, square = column_stats(block)
        mean_e, square_e = edge_stats[g]
        if q:
            mean_e = pltpu.roll(mean_e, 128 - 16 * q, 1)
            square_e = pltpu.roll(square_e, 128 - 16 * q, 1)
        w["mu"][:, s, :128] = mean
        w["mu"][:, s, 128:] = mean_e
        w["sq"][:, s, :128] = square
        w["sq"][:, s, 128:] = square_e

    mu = w["mu"][...]
    sq = w["sq"][...]
    mu0, mu1 = mu[:4].reshape(32, 256), mu[1:].reshape(32, 256)
    sq01 = (sq[:4] + sq[1:]).reshape(32, 256)
    sums = dot_exact(mu0 + mu1, c["means"])
    total = []
    for parity in range(2):
        centre = sums[:, 256 * parity : 256 * parity + 256] * (1.0 / 128)
        d0, d1 = mu0 - centre, mu1 - centre
        total.append(sq01 + 32.0 * (d0 * d0 + d1 * d1))
    variance = dot_exact(jnp.concatenate(total, 1), c["totals"]) * (1.0 / 4096)
    scale = lax.rsqrt(variance + 1e-05) * (1.0 / PATCH)
    if flag is not None:
        scale = scale * flag
    w["scale"][...] = scale.reshape(4, 8, 128)
    centre = jnp.where(lanes((32, 128)) % 32 == 0, sums[:, 512:] * 0.5, 0.0)
    w["centre"][...] = centre.reshape(4, 8, 128)

    w["g32"][...] = jnp.zeros(w["g32"].shape, F32)

    def section(s, carry):
        for pair in range(2):
            columns = []
            for i in (2 * pair, 2 * pair + 1):
                re = w["g"][s, 32 * i : 32 * i + 64, :128] - w["centre"][i, pl.ds(s, 1), :]
                im = w["g"][s, 32 * i : 32 * i + 64, 128:]
                slot = 4 * (s + first) + i
                w["g32"][...] = jnp.where(lane % 32 == slot, pltpu.roll(im, slot, 1), w["g32"][...])
                im = jnp.where(zero_slot, 0.0, im)
                columns.append(jnp.concatenate([re, im], 0).astype(BF16))
            f = dot(c["forward"], jnp.concatenate(columns, 1))
            for n, i in enumerate((2 * pair, 2 * pair + 1)):
                part = f[:, 128 * n : 128 * n + 128] * w["scale"][i, pl.ds(s, 1), :]
                w["f"][s + slot_f, i] = part.astype(BF16)
        return carry

    lax.fori_loop(0, count, section, 0)

    scale32 = jnp.zeros((8, 128), F32)
    sublane = lax.broadcasted_iota(jnp.int32, (8, 128), 0)
    for i in range(4):
        scale32 = scale32 + jnp.where(row_lane % 32 == 4 * (sublane + first) + i, w["scale"][i], 0.0)
    scale32 = jnp.sum(scale32, 0, keepdims=True)
    f = dot(c["forward"][:, :64], w["g32"][...].astype(BF16))
    return (f * scale32).astype(BF16)


def maps(lo, hi, f32, offset, c, w, o_ref):
    f32 = f32.astype(F32)
    re, im = f32[:64], f32[64:]
    for k in range(2):
        re_p = pltpu.roll(re, 128 - 4 * (k + 1), 1)
        im_p = pltpu.roll(im, 128 - 4 * (k + 1), 1)
        q = jnp.concatenate([re * re_p + im * im_p, im * re_p - re * im_p], 0).astype(BF16)
        w["h32"][k] = dot(c["inverse"][:64], q)
    lane = lanes((64, 128))
    zero_slot = lane % 32 == 0
    low = lanes((32, 128)) < 64

    def copy(p):
        return pltpu.make_async_copy(
            w["o"].at[p - lo], o_ref.at[p // 2, p % 2], w["sem"].at[p - lo]
        )

    def pair(p, carry):
        s, k = p // 2, p % 2
        even, odd = [], []
        for half in range(2):
            columns = []
            for i in (2 * half, 2 * half + 1):
                here = w["f"][s - offset, i].astype(F32)
                there = w["f"][s + k + 1 - offset, i].astype(F32)
                f_re, f_im, p_re, p_im = here[:64], here[64:], there[:64], there[64:]
                q = jnp.concatenate([f_re * p_re + f_im * p_im, f_im * p_re - f_re * p_im], 0)
                columns.append(q.astype(BF16))
            h = dot(c["inverse"], jnp.concatenate(columns, 1))
            for n, i in enumerate((2 * half, 2 * half + 1)):
                h_re = h[:64, 128 * n : 128 * n + 128]
                special = pltpu.roll(w["h32"][k], 128 - (4 * s + i), 1)
                h_im = jnp.where(zero_slot, special, h[64:, 128 * n : 128 * n + 128])
                h_cat = jnp.concatenate([h_re, h_im], 1).astype(BF16)
                even.append(h_cat[:32])
                odd.append(h_cat[32:])
        even = dot(jnp.concatenate(even, 0), c["even"])
        odd = dot(jnp.concatenate(odd, 0), c["odd"])
        for i in range(4):
            for half in range(2):
                e = even[32 * i : 32 * i + 32, 128 * half : 128 * half + 128]
                o = odd[32 * i : 32 * i + 32, 128 * half : 128 * half + 128]
                w["mix"][i, pl.ds(2 * half, 32, stride=4), :] = jnp.where(low, e, o)
                w["mix"][i, pl.ds(2 * half + 1, 32, stride=4), :] = pltpu.roll(
                    jnp.where(low, o, e), 64, 1
                )
            w["o"][p - lo, i] = w["mix"][i].astype(BF16)
        copy(p).start()
        return carry

    lax.fori_loop(lo, hi, pair, 0)
    for p in range(lo, hi):
        copy(p).wait()


SCRATCH = dict(
    g=lambda n: pltpu.VMEM((n, 160, 256), F32),
    mu=lambda n: pltpu.VMEM((5, 8, 256), F32),
    sq=lambda n: pltpu.VMEM((5, 8, 256), F32),
    scale=lambda n: pltpu.VMEM((4, 8, 128), F32),
    centre=lambda n: pltpu.VMEM((4, 8, 128), F32),
    g32=lambda n: pltpu.VMEM((64, 128), F32),
    h32=lambda n: pltpu.VMEM((2, 64, 128), F32),
    mix=lambda n: pltpu.VMEM((4, 128, 128), F32),
)


def own_kernel(s_ref, e_ref, ya_ref, yb_ref, t_ref, o_ref, f_ref, f32_ref, *scratch):
    c = Tables(t_ref)
    w = dict(zip((*SCRATCH, "o", "sem"), scratch))
    w["f"] = f_ref
    top, bottom = halo(ya_ref, yb_ref)

    def tall(middle, n):
        return jnp.concatenate([top[16 * n : 16 * n + 16], middle, bottom[16 * n : 16 * n + 16]], 0)

    sections = [tall(s_ref[s], s) for s in range(6)]
    edges = [tall(e_ref[g], 6 + g) for g in range(2)]
    f32 = spectra(6, 0, 0, sections, edges, None, c, w)
    f32_ref[...] = f32
    maps(0, 9, f32, 0, c, w, o_ref)


def rest_kernel(z_ref, h_ref, f_ref, f32_ref, t_ref, _, o_ref, *scratch):
    c = Tables(t_ref)
    w = dict(zip((*SCRATCH, "f", "o", "sem"), scratch))
    flag = jnp.where(lax.axis_index("gz") == 0, 1.0, 0.0)
    w["f"][0] = f_ref[4]
    w["f"][1] = f_ref[5]
    tall = [
        jnp.concatenate([h_ref[16 * n : 16 * n + 16], z_ref[n], h_ref[48 + 16 * n : 64 + 16 * n]], 0)
        for n in range(3)
    ]
    extra = spectra(2, 6, 2, tall[:2], tall[2:], flag, c, w)
    f32 = jnp.where(lanes((128, 128)) % 32 >= 24, extra.astype(F32), f32_ref[...].astype(F32))
    maps(9, 12, f32, 4, c, w, o_ref)


def exchange(value_a, value_b, axis, count):
    pairs_a = [(n, n ^ 1) for n in range(count)]
    pairs_b = [(n, n + 1 if n % 2 else n - 1) for n in range(1, count - 1)]
    return lax.ppermute(value_a, axis, pairs_a), lax.ppermute(value_b, axis, pairs_b)


def other(value):
    return lax.ppermute(value, "gz", [(0, 1), (1, 0)])


def shaped(*shape):
    return jax.ShapeDtypeStruct(shape, BF16)


def params(mib):
    return pltpu.CompilerParams(vmem_limit_bytes=mib * 2**20)


def local(sections):
    edge = shaped(128, 128)
    fixed = [pltpu.with_memory_space_constraint(value, pltpu.HBM) for value in (sections, constants()[0])]
    xa, xb, sections, table = pl.pallas_call(
        edges_kernel,
        out_shape=(edge, edge, *(shaped(*value.shape) for value in fixed)),
        in_specs=[HBM] * 2,
        out_specs=(VMEM,) * 4,
        scratch_shapes=[pltpu.SemaphoreType.DMA((2,))],
        compiler_params=params(8),
    )(*fixed)
    xa, xb = exchange(xa, xb, "gx", lax.axis_size("gx"))
    edges, ya, yb, z = pl.pallas_call(
        rows_kernel,
        out_shape=(shaped(2, 128, 128), edge, edge, shaped(3, 128, 128)),
        in_specs=[VMEM] * 3,
        out_specs=(VMEM,) * 4,
        compiler_params=params(8),
    )(sections, xa, xb)
    ya, yb = exchange(ya, yb, "gy", lax.axis_size("gy"))
    z = other(z)
    rows = pl.pallas_call(
        halo_kernel,
        out_shape=shaped(96, 128),
        in_specs=[VMEM] * 2,
        out_specs=VMEM,
        compiler_params=params(8),
    )(ya, yb)
    rows = other(rows)
    scratch = [make(6) for make in SCRATCH.values()]
    out, f, f32 = pl.pallas_call(
        own_kernel,
        out_shape=(shaped(6, 2, 4, 128, 128), shaped(6, 4, 128, 128), edge),
        in_specs=[VMEM] * 5,
        out_specs=(HBM, VMEM, VMEM),
        scratch_shapes=scratch + [pltpu.VMEM((9, 4, 128, 128), BF16), pltpu.SemaphoreType.DMA((9,))],
        compiler_params=params(16),
        cost_estimate=pl.CostEstimate(flops=10**9, bytes_accessed=4 * 10**6, transcendentals=0),
    )(sections, edges, ya, yb, table)
    scratch = [make(2) for make in SCRATCH.values()]
    out = pl.pallas_call(
        rest_kernel,
        out_shape=shaped(6, 2, 4, 128, 128),
        in_specs=[VMEM] * 5 + [HBM],
        out_specs=HBM,
        scratch_shapes=scratch
        + [
            pltpu.VMEM((4, 4, 128, 128), BF16),
            pltpu.VMEM((3, 4, 128, 128), BF16),
            pltpu.SemaphoreType.DMA((3,)),
        ],
        input_output_aliases={5: 0},
        compiler_params=params(16),
    )(z, rows, f, f32, table, out)
    out = out.reshape(6, 2, 4, 32, 4, 128).transpose(0, 1, 2, 4, 3, 5)
    return out.reshape(6, 2, 4, 4, 4096)


def solution(mesh):
    return jax.shard_map(
        local,
        mesh=mesh,
        in_specs=(P("gz", "gy", "gx"),),
        out_specs=P("gz", None, "gy", "gx", None),
        check_vma=False,
    )
```

```python
import functools
import math

import jax
import jax.numpy as jnp
import ml_dtypes
import numpy as np
from jax import lax
from jax.experimental import pallas as pl
from jax.experimental.pallas import tpu as pltpu
from jax.sharding import PartitionSpec as P

PATCH = 64
AXES = ("gx", "gy", "gz")
F32 = jnp.float32
BF16 = jnp.bfloat16
VMEM = pl.BlockSpec(memory_space=pltpu.VMEM)
HBM = pl.BlockSpec(memory_space=pltpu.HBM)


def rounded(values):
    return values.astype(np.float32).astype(ml_dtypes.bfloat16)


@functools.cache
def constants():
    index = np.arange(PATCH)
    angle = (index[:, None] * index[None, :] % PATCH) * (2.0 * math.pi / PATCH)
    cos = rounded(np.cos(angle)).astype(np.float64)
    sin = rounded(np.sin(angle)).astype(np.float64)
    sign = 1.0 - 2.0 * (index % 2)

    rows = np.zeros((160, 2, 4, 32))
    for j in range(4):
        rows[32 * j : 32 * j + 64, 0, j] = cos[:, :32]
        rows[32 * j : 32 * j + 64, 1, j] = -sin[:, :32]
        rows[32 * j : 32 * j + 64, 1, j, 0] = sign
    rows = rows.reshape(160, 256)

    forward = np.block([[cos, sin], [-sin, cos]])
    order = np.concatenate([index[0::2], index[1::2]])
    inverse = np.block([[cos[order], -sin[order]], [sin[order], cos[order]]])

    last = np.zeros((2, 4, 32, 4, 64))
    weight = np.where(index[:32] == 0, 1.0, 2.0)[:, None] / 4096.0
    for j in range(4):
        last[0, j, :, j] = weight * cos[:32]
        last[1, j, :, j] = -weight * sin[:32]
        last[1, j, 0, j] = sign / 4096.0
    even = last.reshape(256, 256)
    odd = last[:, :, :, [1, 0, 3, 2]].reshape(256, 256)

    column = np.full(256, -1000)
    column[:128] = np.arange(128) + 16
    column[128:144] = np.arange(16)
    column[192:208] = np.arange(16) + 144
    inside = np.stack([(column >= 32 * j) & (column < 32 * j + 64) for j in range(4)], 1)
    inside = inside.astype(np.float64)
    same_even = inside[:, [0, 2]] @ inside[:, [0, 2]].T
    same_odd = inside[:, [1, 3]] @ inside[:, [1, 3]].T
    spread = np.repeat(inside, 32, axis=1)
    lane_odd = (np.arange(128) // 32 % 2).astype(np.float64)
    means = np.concatenate([same_even, same_odd, spread], 1)
    totals = np.concatenate([spread * (1 - lane_odd), spread * lane_odd], 0)
    tables = dict(
        own=rows[16:144],
        sides=np.concatenate([rows[:16], rows[144:]], 0),
        forward=forward,
        inverse=inverse,
        even=even,
        odd=odd,
        means=means,
        totals=totals,
    )
    pieces, places, at = [], {}, 0
    for name, table in tables.items():
        height, width = table.shape
        places[name] = (at, height, width // 128)
        pieces += np.split(table, width // 128, 1)
        at += height * width // 128
    return rounded(np.concatenate(pieces, 0)), places


class Tables:
    def __init__(self, ref):
        self.ref = ref

    def __getitem__(self, name):
        at, height, width = constants()[1][name]
        pieces = [self.ref[at + height * n : at + height * (n + 1)] for n in range(width)]
        return jnp.concatenate(pieces, 1) if width > 1 else pieces[0]


def dot(a, b):
    return jnp.dot(a, b, preferred_element_type=F32)


def dot_exact(a, ones):
    high = a.astype(BF16)
    rest = a - high.astype(F32)
    middle = rest.astype(BF16)
    low = (rest - middle.astype(F32)).astype(BF16)
    n = a.shape[0]
    parts = dot(jnp.concatenate([high, middle, low], 0), ones)
    return parts[2 * n :] + parts[n : 2 * n] + parts[:n]


def lanes(shape):
    return lax.broadcasted_iota(jnp.int32, shape, len(shape) - 1)


def edges_kernel(s_hbm, t_hbm, a_ref, b_ref, s_ref, t_ref, sem):
    sections = pltpu.make_async_copy(s_hbm, s_ref, sem.at[0])
    tables = pltpu.make_async_copy(t_hbm, t_ref, sem.at[1])
    sections.start()
    tables.start()
    sections.wait()
    odd = lax.axis_index("gx") % 2 == 1
    lane = lanes((128, 128))
    left = jnp.zeros((128, 128), F32)
    right = jnp.zeros((128, 128), F32)
    for s in range(6):
        block = s_ref[s].astype(F32)
        here = (lane // 16) == s
        first = pltpu.roll(block, 16 * s, 1) if s else block
        last = pltpu.roll(block, 16 * s + 16, 1)
        left = jnp.where(here, first, left)
        right = jnp.where(here, last, right)
    a_ref[...] = jnp.where(odd, left, right).astype(BF16)
    b_ref[...] = jnp.where(odd, right, left).astype(BF16)
    tables.wait()


def rows_kernel(s_ref, xa_ref, xb_ref, e_ref, a_ref, b_ref, z_ref):
    odd_y = lax.axis_index("gy") % 2 == 1
    left, right = low_high(xa_ref[...], xb_ref[...], "gx")
    left, right = left.astype(F32), right.astype(F32)
    low = lanes((128, 128)) < 64
    e0 = jnp.where(low, left, pltpu.roll(right, 64, 1)).astype(BF16)
    e1 = jnp.where(low, pltpu.roll(left, 64, 1), right).astype(BF16)
    e_ref[0] = e0
    e_ref[1] = e1
    first = jnp.concatenate([s_ref[s, :16] for s in range(6)] + [e0[:16], e1[:16]], 0)
    last = jnp.concatenate([s_ref[s, 112:] for s in range(6)] + [e0[112:], e1[112:]], 0)
    a_ref[...] = jnp.where(odd_y, first, last)
    b_ref[...] = jnp.where(odd_y, last, first)
    z_ref[0] = s_ref[0]
    z_ref[1] = s_ref[1]
    z_ref[2] = e0


def halo_kernel(ya_ref, yb_ref, z_ref):
    top, bottom = low_high(ya_ref[...], yb_ref[...], "gy")
    for n, at in enumerate((0, 16, 96)):
        z_ref[16 * n : 16 * n + 16] = top[at : at + 16]
        z_ref[48 + 16 * n : 64 + 16 * n] = bottom[at : at + 16]


def low_high(a, b, axis):
    at = lax.axis_index(axis)
    odd = at % 2 == 1
    zero = jnp.zeros_like(a)
    low = jnp.where(odd, a, jnp.where(at == 0, zero, b))
    high = jnp.where(odd, jnp.where(at == lax.axis_size(axis) - 1, zero, b), a)
    return low, high


def spectra(count, first, slot_f, sections, edges, flag, c, w):
    lane = lanes((64, 128))
    zero_slot = lane % 32 == 0
    row_lane = lanes((8, 128))
    sides = c["sides"]
    def column_stats(block):
        block = block.astype(F32).reshape(5, 32, 128)
        mean = jnp.sum(block, 1, keepdims=True) * (1.0 / 32)
        centred = block - mean
        return mean[:, 0], jnp.sum(centred * centred, 1)

    edge_stats = [column_stats(g) for g in edges]
    w["mu"][...] = jnp.zeros(w["mu"].shape, F32)
    w["sq"][...] = jnp.zeros(w["sq"].shape, F32)
    for s in range(count):
        q, g = s % 4, s // 4
        block = sections[s]
        gap0 = jnp.zeros((16 * q, 256), BF16)
        gap1 = jnp.zeros((48 - 16 * q, 256), BF16)
        pieces = [c["own"], gap0, sides[:16], gap1, gap0, sides[16:], gap1]
        table = jnp.concatenate([p for p in pieces if p.shape[0]], 0)
        w["g"][s] = dot(jnp.concatenate([block, edges[g]], 1), table)
        mean, square = column_stats(block)
        mean_e, square_e = edge_stats[g]
        if q:
            mean_e = pltpu.roll(mean_e, 128 - 16 * q, 1)
            square_e = pltpu.roll(square_e, 128 - 16 * q, 1)
        w["mu"][:, s, :128] = mean
        w["mu"][:, s, 128:] = mean_e
        w["sq"][:, s, :128] = square
        w["sq"][:, s, 128:] = square_e

    mu = w["mu"][...]
    sq = w["sq"][...]
    mu0, mu1 = mu[:4].reshape(32, 256), mu[1:].reshape(32, 256)
    sq01 = (sq[:4] + sq[1:]).reshape(32, 256)
    sums = dot_exact(mu0 + mu1, c["means"])
    total = []
    for parity in range(2):
        centre = sums[:, 256 * parity : 256 * parity + 256] * (1.0 / 128)
        d0, d1 = mu0 - centre, mu1 - centre
        total.append(sq01 + 32.0 * (d0 * d0 + d1 * d1))
    variance = dot_exact(jnp.concatenate(total, 1), c["totals"]) * (1.0 / 4096)
    scale = lax.rsqrt(variance + 1e-05) * (1.0 / PATCH)
    if flag is not None:
        scale = scale * flag
    w["scale"][...] = scale.reshape(4, 8, 128)
    centre = jnp.where(lanes((32, 128)) % 32 == 0, sums[:, 512:] * 0.5, 0.0)
    w["centre"][...] = centre.reshape(4, 8, 128)

    w["g32"][...] = jnp.zeros(w["g32"].shape, F32)

    def section(s):
        for pair in range(2):
            columns = []
            for i in (2 * pair, 2 * pair + 1):
                re = w["g"][s, 32 * i : 32 * i + 64, :128] - w["centre"][i, s : s + 1, :]
                im = w["g"][s, 32 * i : 32 * i + 64, 128:]
                slot = 4 * (s + first) + i
                w["g32"][...] = jnp.where(lane % 32 == slot, (pltpu.roll(im, slot, 1) if slot else im), w["g32"][...])
                im = jnp.where(zero_slot, 0.0, im)
                columns.append(jnp.concatenate([re, im], 0).astype(BF16))
            f = dot(c["forward"], jnp.concatenate(columns, 1))
            for n, i in enumerate((2 * pair, 2 * pair + 1)):
                part = f[:, 128 * n : 128 * n + 128] * w["scale"][i, s : s + 1, :]
                w["f"][s + slot_f, i] = part.astype(BF16)

    for s in range(count):
        section(s)

    scale32 = jnp.zeros((8, 128), F32)
    sublane = lax.broadcasted_iota(jnp.int32, (8, 128), 0)
    for i in range(4):
        scale32 = scale32 + jnp.where(row_lane % 32 == 4 * (sublane + first) + i, w["scale"][i], 0.0)
    scale32 = jnp.sum(scale32, 0, keepdims=True)
    f = dot(c["forward"][:, :64], w["g32"][...].astype(BF16))
    return (f * scale32).astype(BF16)


def maps(lo, hi, f32, offset, c, w, o_ref):
    f32 = f32.astype(F32)
    re, im = f32[:64], f32[64:]
    for k in range(2):
        re_p = pltpu.roll(re, 128 - 4 * (k + 1), 1)
        im_p = pltpu.roll(im, 128 - 4 * (k + 1), 1)
        q = jnp.concatenate([re * re_p + im * im_p, im * re_p - re * im_p], 0).astype(BF16)
        w["h32"][k] = dot(c["inverse"][:64], q)
    lane = lanes((64, 128))
    zero_slot = lane % 32 == 0
    low = lanes((32, 128)) < 64

    def copy(p):
        return pltpu.make_async_copy(
            w["o"].at[p - lo], o_ref.at[p // 2, p % 2], w["sem"].at[p - lo]
        )

    def pair(p):
        s, k = p // 2, p % 2
        even, odd = [], []
        for half in range(2):
            columns = []
            for i in (2 * half, 2 * half + 1):
                here = w["f"][s - offset, i].astype(F32)
                there = w["f"][s + k + 1 - offset, i].astype(F32)
                f_re, f_im, p_re, p_im = here[:64], here[64:], there[:64], there[64:]
                q = jnp.concatenate([f_re * p_re + f_im * p_im, f_im * p_re - f_re * p_im], 0)
                columns.append(q.astype(BF16))
            h = dot(c["inverse"], jnp.concatenate(columns, 1))
            for n, i in enumerate((2 * half, 2 * half + 1)):
                h_re = h[:64, 128 * n : 128 * n + 128]
                special = pltpu.roll(w["h32"][k], (128 - 4 * s - i) % 128, 1)
                h_im = jnp.where(zero_slot, special, h[64:, 128 * n : 128 * n + 128])
                h_cat = jnp.concatenate([h_re, h_im], 1).astype(BF16)
                even.append(h_cat[:32])
                odd.append(h_cat[32:])
        even = dot(jnp.concatenate(even, 0), c["even"])
        odd = dot(jnp.concatenate(odd, 0), c["odd"])
        for i in range(4):
            for half in range(2):
                e = even[32 * i : 32 * i + 32, 128 * half : 128 * half + 128]
                o = odd[32 * i : 32 * i + 32, 128 * half : 128 * half + 128]
                w["mix"][i, pl.ds(2 * half, 32, stride=4), :] = jnp.where(low, e, o)
                w["mix"][i, pl.ds(2 * half + 1, 32, stride=4), :] = pltpu.roll(
                    jnp.where(low, o, e), 64, 1
                )
            w["o"][p - lo, i] = w["mix"][i].astype(BF16)
        copy(p).start()

    for p in range(lo, hi):
        pair(p)
    for p in range(lo, hi):
        copy(p).wait()


SCRATCH = dict(
    g=lambda n: pltpu.VMEM((n, 160, 256), F32),
    mu=lambda n: pltpu.VMEM((5, 8, 256), F32),
    sq=lambda n: pltpu.VMEM((5, 8, 256), F32),
    scale=lambda n: pltpu.VMEM((4, 8, 128), F32),
    centre=lambda n: pltpu.VMEM((4, 8, 128), F32),
    g32=lambda n: pltpu.VMEM((64, 128), F32),
    h32=lambda n: pltpu.VMEM((2, 64, 128), F32),
    mix=lambda n: pltpu.VMEM((4, 128, 128), F32),
)


def own_kernel(s_ref, e_ref, ya_ref, yb_ref, t_ref, o_ref, f_ref, f32_ref, *scratch):
    c = Tables(t_ref)
    w = dict(zip((*SCRATCH, "o", "sem"), scratch))
    w["f"] = f_ref
    top, bottom = low_high(ya_ref[...], yb_ref[...], "gy")

    def tall(middle, n):
        return jnp.concatenate([top[16 * n : 16 * n + 16], middle, bottom[16 * n : 16 * n + 16]], 0)

    sections = [tall(s_ref[s], s) for s in range(6)]
    edges = [tall(e_ref[g], 6 + g) for g in range(2)]
    f32 = spectra(6, 0, 0, sections, edges, None, c, w)
    f32_ref[...] = f32
    maps(0, 9, f32, 0, c, w, o_ref)


def rest_kernel(z_ref, h_ref, f_ref, f32_ref, t_ref, _, o_ref, *scratch):
    c = Tables(t_ref)
    w = dict(zip((*SCRATCH, "f", "o", "sem"), scratch))
    flag = jnp.where(lax.axis_index("gz") == 0, 1.0, 0.0)
    w["f"][0] = f_ref[4]
    w["f"][1] = f_ref[5]
    tall = [
        jnp.concatenate([h_ref[16 * n : 16 * n + 16], z_ref[n], h_ref[48 + 16 * n : 64 + 16 * n]], 0)
        for n in range(3)
    ]
    extra = spectra(2, 6, 2, tall[:2], tall[2:], flag, c, w)
    f32 = jnp.where(lanes((128, 128)) % 32 >= 24, extra.astype(F32), f32_ref[...].astype(F32))
    maps(9, 12, f32, 4, c, w, o_ref)


def exchange(value_a, value_b, axis):
    sizes = [lax.axis_size(name) for name in AXES]
    along, across = AXES.index(axis), 1 - AXES.index(axis)

    def partner(place, first):
        place = list(place)
        up = place[along] % 2 == first
        moved = place[along] + (1 if up else -1)
        if 0 <= moved < sizes[along]:
            place[along] = moved
        else:
            place[across] ^= 1
        return place

    def pairs(first):
        return [
            (int(np.ravel_multi_index(at, sizes)), int(np.ravel_multi_index(partner(at, first), sizes)))
            for at in np.ndindex(*sizes)
        ]

    return lax.ppermute(value_a, AXES, pairs(0)), lax.ppermute(value_b, AXES, pairs(1))


def other(value):
    return lax.ppermute(value, "gz", [(0, 1), (1, 0)])


def shaped(*shape):
    return jax.ShapeDtypeStruct(shape, BF16)


def params(mib):
    return pltpu.CompilerParams(vmem_limit_bytes=mib * 2**20)


def local(sections):
    edge = shaped(128, 128)
    fixed = [pltpu.with_memory_space_constraint(value, pltpu.HBM) for value in (sections, constants()[0])]
    xa, xb, sections, table = pl.pallas_call(
        edges_kernel,
        out_shape=(edge, edge, *(shaped(*value.shape) for value in fixed)),
        in_specs=[HBM] * 2,
        out_specs=(VMEM,) * 4,
        scratch_shapes=[pltpu.SemaphoreType.DMA((2,))],
        compiler_params=params(8),
    )(*fixed)
    xa, xb = exchange(xa, xb, "gx")
    edges, ya, yb, z = pl.pallas_call(
        rows_kernel,
        out_shape=(shaped(2, 128, 128), edge, edge, shaped(3, 128, 128)),
        in_specs=[VMEM] * 3,
        out_specs=(VMEM,) * 4,
        compiler_params=params(8),
    )(sections, xa, xb)
    ya, yb = exchange(ya, yb, "gy")
    z = other(z)
    rows = pl.pallas_call(
        halo_kernel,
        out_shape=shaped(96, 128),
        in_specs=[VMEM] * 2,
        out_specs=VMEM,
        compiler_params=params(8),
    )(ya, yb)
    rows = other(rows)
    scratch = [make(6) for make in SCRATCH.values()]
    out, f, f32 = pl.pallas_call(
        own_kernel,
        out_shape=(shaped(6, 2, 4, 128, 128), shaped(6, 4, 128, 128), edge),
        in_specs=[VMEM] * 5,
        out_specs=(HBM, VMEM, VMEM),
        scratch_shapes=scratch + [pltpu.VMEM((9, 4, 128, 128), BF16), pltpu.SemaphoreType.DMA((9,))],
        compiler_params=params(16),
        cost_estimate=pl.CostEstimate(flops=10**9, bytes_accessed=4 * 10**6, transcendentals=0),
    )(sections, edges, ya, yb, table)
    scratch = [make(2) for make in SCRATCH.values()]
    out = pl.pallas_call(
        rest_kernel,
        out_shape=shaped(6, 2, 4, 128, 128),
        in_specs=[VMEM] * 5 + [HBM],
        out_specs=HBM,
        scratch_shapes=scratch
        + [
            pltpu.VMEM((4, 4, 128, 128), BF16),
            pltpu.VMEM((3, 4, 128, 128), BF16),
            pltpu.SemaphoreType.DMA((3,)),
        ],
        input_output_aliases={5: 0},
        compiler_params=params(16),
    )(z, rows, f, f32, table, out)
    out = out.reshape(6, 2, 4, 32, 4, 128).transpose(0, 1, 2, 4, 3, 5)
    return out.reshape(6, 2, 4, 4, 4096)


def solution(mesh):
    return jax.shard_map(
        local,
        mesh=mesh,
        in_specs=(P("gz", "gy", "gx"),),
        out_specs=P("gz", None, "gy", "gx", None),
        check_vma=False,
    )
```

```python
import functools
import math

import jax
import jax.numpy as jnp
import ml_dtypes
import numpy as np
from jax import lax
from jax.experimental import pallas as pl
from jax.experimental.pallas import tpu as pltpu
from jax.sharding import PartitionSpec as P

PATCH = 64
AXES = ("gx", "gy", "gz")
F32 = jnp.float32
BF16 = jnp.bfloat16
VMEM = pl.BlockSpec(memory_space=pltpu.VMEM)
HBM = pl.BlockSpec(memory_space=pltpu.HBM)


def rounded(values):
    return values.astype(np.float32).astype(ml_dtypes.bfloat16)


@functools.cache
def constants():
    index = np.arange(PATCH)
    angle = (index[:, None] * index[None, :] % PATCH) * (2.0 * math.pi / PATCH)
    cos = rounded(np.cos(angle)).astype(np.float64)
    sin = rounded(np.sin(angle)).astype(np.float64)
    sign = 1.0 - 2.0 * (index % 2)

    rows = np.zeros((160, 2, 4, 32))
    for j in range(4):
        rows[32 * j : 32 * j + 64, 0, j] = cos[:, :32]
        rows[32 * j : 32 * j + 64, 1, j] = -sin[:, :32]
        rows[32 * j : 32 * j + 64, 1, j, 0] = sign
    rows = rows.reshape(160, 256)

    forward = np.block([[cos, sin], [-sin, cos]])
    order = np.concatenate([index[0::2], index[1::2]])
    inverse = np.block([[cos[order], -sin[order]], [sin[order], cos[order]]])

    last = np.zeros((2, 4, 32, 4, 64))
    weight = np.where(index[:32] == 0, 1.0, 2.0)[:, None] / 4096.0
    for j in range(4):
        last[0, j, :, j] = weight * cos[:32]
        last[1, j, :, j] = -weight * sin[:32]
        last[1, j, 0, j] = sign / 4096.0
    even = last.reshape(256, 256)
    odd = last[:, :, :, [1, 0, 3, 2]].reshape(256, 256)

    column = np.full(256, -1000)
    column[:128] = np.arange(128) + 16
    column[128:144] = np.arange(16)
    column[192:208] = np.arange(16) + 144
    inside = np.stack([(column >= 32 * j) & (column < 32 * j + 64) for j in range(4)], 1)
    inside = inside.astype(np.float64)
    same_even = inside[:, [0, 2]] @ inside[:, [0, 2]].T
    same_odd = inside[:, [1, 3]] @ inside[:, [1, 3]].T
    spread = np.repeat(inside, 64, axis=1)
    lane_odd = (np.arange(256) // 64 % 2).astype(np.float64)
    means = np.concatenate([same_even, same_odd], 1)
    totals = np.concatenate([spread * (1 - lane_odd), spread * lane_odd], 0)
    tables = dict(
        own=rows[16:144],
        sides=np.concatenate([rows[:16], rows[144:]], 0),
        forward=forward,
        inverse=inverse,
        even=even,
        odd=odd,
        means=means,
        totals=totals,
    )
    pieces, places, at = [], {}, 0
    for name, table in tables.items():
        height, width = table.shape
        places[name] = (at, height, width // 128)
        pieces += np.split(table, width // 128, 1)
        at += height * width // 128
    return rounded(np.concatenate(pieces, 0)), places


class Tables:
    def __init__(self, ref):
        self.ref = ref

    def __getitem__(self, name):
        at, height, width = constants()[1][name]
        pieces = [self.ref[at + height * n : at + height * (n + 1)] for n in range(width)]
        return jnp.concatenate(pieces, 1) if width > 1 else pieces[0]


def dot(a, b):
    return jnp.dot(a, b, preferred_element_type=F32)


def dot_exact(a, ones):
    high = a.astype(BF16)
    rest = a - high.astype(F32)
    middle = rest.astype(BF16)
    low = (rest - middle.astype(F32)).astype(BF16)
    n = a.shape[0]
    parts = dot(jnp.concatenate([high, middle, low], 0), ones)
    return parts[2 * n :] + parts[n : 2 * n] + parts[:n]


def lanes(shape):
    return lax.broadcasted_iota(jnp.int32, shape, len(shape) - 1)


def edges_kernel(s_hbm, t_hbm, a_ref, b_ref, s_ref, t_ref, sem):
    sections = pltpu.make_async_copy(s_hbm, s_ref, sem.at[0])
    tables = pltpu.make_async_copy(t_hbm, t_ref, sem.at[1])
    sections.start()
    tables.start()
    sections.wait()
    odd = lax.axis_index("gx") % 2 == 1
    lane = lanes((128, 128))
    left = jnp.zeros((128, 128), F32)
    right = jnp.zeros((128, 128), F32)
    for s in range(6):
        block = s_ref[s].astype(F32)
        here = (lane // 16) == s
        first = pltpu.roll(block, 16 * s, 1) if s else block
        last = pltpu.roll(block, 16 * s + 16, 1)
        left = jnp.where(here, first, left)
        right = jnp.where(here, last, right)
    a_ref[...] = jnp.where(odd, left, right).astype(BF16)
    b_ref[...] = jnp.where(odd, right, left).astype(BF16)
    tables.wait()


def rows_kernel(s_ref, xa_ref, xb_ref, e_ref, a_ref, b_ref, z_ref):
    odd_y = lax.axis_index("gy") % 2 == 1
    left, right = low_high(xa_ref[...], xb_ref[...], "gx")
    left, right = left.astype(F32), right.astype(F32)
    low = lanes((128, 128)) < 64
    e0 = jnp.where(low, left, pltpu.roll(right, 64, 1)).astype(BF16)
    e1 = jnp.where(low, pltpu.roll(left, 64, 1), right).astype(BF16)
    e_ref[0] = e0
    e_ref[1] = e1
    first = jnp.concatenate([s_ref[s, :16] for s in range(6)] + [e0[:16], e1[:16]], 0)
    last = jnp.concatenate([s_ref[s, 112:] for s in range(6)] + [e0[112:], e1[112:]], 0)
    a_ref[...] = jnp.where(odd_y, first, last)
    b_ref[...] = jnp.where(odd_y, last, first)
    z_ref[0] = s_ref[0]
    z_ref[1] = s_ref[1]
    z_ref[2] = e0


def halo_kernel(ya_ref, yb_ref, z_ref):
    top, bottom = low_high(ya_ref[...], yb_ref[...], "gy")
    for n, at in enumerate((0, 16, 96)):
        z_ref[16 * n : 16 * n + 16] = top[at : at + 16]
        z_ref[48 + 16 * n : 64 + 16 * n] = bottom[at : at + 16]


def low_high(a, b, axis):
    at = lax.axis_index(axis)
    odd = at % 2 == 1
    zero = jnp.zeros_like(a)
    low = jnp.where(odd, a, jnp.where(at == 0, zero, b))
    high = jnp.where(odd, jnp.where(at == lax.axis_size(axis) - 1, zero, b), a)
    return low, high


def column_stats(block):
    block = block.astype(F32).reshape(5, 32, 128)
    mean = jnp.sum(block, 1, keepdims=True) * (1.0 / 32)
    centred = block - mean
    return mean[:, 0], jnp.sum(centred * centred, 1)


def scales(first, sections, edges, c, w):
    edge_stats = [column_stats(g) for g in edges]
    w["mu"][...] = jnp.zeros(w["mu"].shape, F32)
    w["sq"][...] = jnp.zeros(w["sq"].shape, F32)
    for s, block in enumerate(sections):
        q, g = s % 4, s // 4
        mean, square = column_stats(block)
        mean_e, square_e = edge_stats[g]
        if q:
            mean_e = pltpu.roll(mean_e, 128 - 16 * q, 1)
            square_e = pltpu.roll(square_e, 128 - 16 * q, 1)
        w["mu"][:, first + s, :128] = mean
        w["mu"][:, first + s, 128:] = mean_e
        w["sq"][:, first + s, :128] = square
        w["sq"][:, first + s, 128:] = square_e
    mu = w["mu"][...]
    sq = w["sq"][...]
    mu0, mu1 = mu[:4].reshape(32, 256), mu[1:].reshape(32, 256)
    sq01 = (sq[:4] + sq[1:]).reshape(32, 256)
    sums = dot_exact(mu0 + mu1, c["means"])
    total = []
    for parity in range(2):
        centre = sums[:, 256 * parity : 256 * parity + 256] * (1.0 / 128)
        d0, d1 = mu0 - centre, mu1 - centre
        total.append(sq01 + 32.0 * (d0 * d0 + d1 * d1))
    variance = dot_exact(jnp.concatenate(total, 1), c["totals"]) * (1.0 / 4096)
    return lax.rsqrt(variance + 1e-05) * (1.0 / PATCH)


def store_scales(scale, w):
    for half in range(2):
        part = scale[:, 128 * half : 128 * half + 128]
        w["scale"][0, half] = part.reshape(4, 8, 128)
        w["scale"][1, half] = pltpu.roll(part, 64, 1).reshape(4, 8, 128)


def spectra(first, slot_f, sections, edges, c, w):
    lane = lanes((64, 128))
    zero_slot = lane % 32 == 0
    sides = c["sides"]
    for s, block in enumerate(sections):
        q = s % 4
        gap0 = jnp.zeros((16 * q, 256), BF16)
        gap1 = jnp.zeros((48 - 16 * q, 256), BF16)
        pieces = [c["own"], gap0, sides[:16], gap1, gap0, sides[16:], gap1]
        table = jnp.concatenate([p for p in pieces if p.shape[0]], 0)
        w["g"][s] = dot(jnp.concatenate([block, edges[s // 4]], 1), table)
    special = jnp.zeros((64, 128), F32)
    for s in range(len(sections)):
        for pair in range(2):
            columns = []
            for i in (2 * pair, 2 * pair + 1):
                re = w["g"][s, 32 * i : 32 * i + 64, :128]
                im = w["g"][s, 32 * i : 32 * i + 64, 128:]
                centre = jnp.sum(re, 0, keepdims=True) * (1.0 / 64)
                re = jnp.where(zero_slot, re - centre, re)
                slot = 4 * (s + first) + i
                special = jnp.where(lane % 32 == slot, pltpu.roll(im, slot, 1) if slot else im, special)
                im = jnp.where(zero_slot, 0.0, im)
                columns.append(jnp.concatenate([re, im], 0).astype(BF16))
            f = dot(c["forward"], jnp.concatenate(columns, 1)).astype(BF16)
            for n, i in enumerate((2 * pair, 2 * pair + 1)):
                w["f"][s + slot_f, i] = f[:, 128 * n : 128 * n + 128]
    return dot(c["forward"][:, :64], special.astype(BF16)).astype(BF16)


def maps(lo, hi, f32, offset, c, w, o_ref):
    lane = lanes((64, 128))
    zero_slot = lane % 32 == 0
    low = lanes((32, 128)) < 64
    f32 = f32.astype(F32)
    re, im = f32[:64], f32[64:]
    h32 = []
    for k in range(2):
        re_p = pltpu.roll(re, 128 - 4 * (k + 1), 1)
        im_p = pltpu.roll(im, 128 - 4 * (k + 1), 1)
        q = jnp.concatenate([re * re_p + im * im_p, im * re_p - re * im_p], 0).astype(BF16)
        h32.append(dot(c["inverse"][:64], q))

    def copy(p):
        return pltpu.make_async_copy(
            w["o"].at[p - lo], o_ref.at[p // 2, p % 2], w["sem"].at[p - lo]
        )

    def correlate(p):
        s, k = p // 2, p % 2
        spectra = []
        for half in range(2):
            columns = []
            for i in (2 * half, 2 * half + 1):
                here = w["f"][s - offset, i].astype(F32)
                there = w["f"][s + k + 1 - offset, i].astype(F32)
                f_re, f_im, p_re, p_im = here[:64], here[64:], there[:64], there[64:]
                q = jnp.concatenate([f_re * p_re + f_im * p_im, f_im * p_re - f_re * p_im], 0)
                columns.append(q.astype(BF16))
            spectra.append(dot(c["inverse"], jnp.concatenate(columns, 1)))
        return spectra

    def last(p, spectra):
        s, k = p // 2, p % 2
        even, odd = [], []
        for i in range(4):
            h = spectra[i // 2][:, 128 * (i % 2) : 128 * (i % 2) + 128]
            special = pltpu.roll(h32[k], (128 - 4 * s - i) % 128, 1)
            h_im = jnp.where(zero_slot, special, h[64:])
            h_cat = jnp.concatenate([h[:64], h_im], 1).astype(BF16)
            even.append(h_cat[:32])
            odd.append(h_cat[32:])
        even = dot(jnp.concatenate(even, 0), c["even"])
        odd = dot(jnp.concatenate(odd, 0), c["odd"])
        return even, odd

    def store(p, even, odd):
        s, k = p // 2, p % 2
        mix = w["mix"].at[p % 2]
        for i in range(4):
            for half in range(2):
                e_scale, o_scale = [
                    w["scale"][n, half, i, s : s + 1] * w["scale"][n, half, i, s + k + 1 : s + k + 2]
                    for n in range(2)
                ]
                e = even[32 * i : 32 * i + 32, 128 * half : 128 * half + 128] * e_scale
                o = odd[32 * i : 32 * i + 32, 128 * half : 128 * half + 128] * o_scale
                mix[i, pl.ds(2 * half, 32, stride=4), :] = jnp.where(low, e, o)
                mix[i, pl.ds(2 * half + 1, 32, stride=4), :] = pltpu.roll(jnp.where(low, o, e), 64, 1)
            w["o"][p - lo, i] = mix[i].astype(BF16)
        copy(p).start()

    ready = correlate(lo)
    for p in range(lo, hi):
        following = correlate(p + 1) if p + 1 < hi else None
        store(p, *last(p, ready))
        ready = following
    for p in range(lo, hi):
        copy(p).wait()


SCRATCH = dict(
    g=lambda n: pltpu.VMEM((n, 160, 256), F32),
    mu=lambda n: pltpu.VMEM((5, 8, 256), F32),
    sq=lambda n: pltpu.VMEM((5, 8, 256), F32),
    scale=lambda n: pltpu.VMEM((2, 2, 4, 8, 128), F32),
    mix=lambda n: pltpu.VMEM((2, 4, 128, 128), F32),
)


def own_kernel(s_ref, e_ref, ya_ref, yb_ref, t_ref, o_ref, f_ref, f32_ref, scale_ref, *scratch):
    c = Tables(t_ref)
    w = dict(zip((*SCRATCH, "o", "sem"), scratch))
    w["f"] = f_ref
    top, bottom = low_high(ya_ref[...], yb_ref[...], "gy")

    def tall(middle, n):
        return jnp.concatenate([top[16 * n : 16 * n + 16], middle, bottom[16 * n : 16 * n + 16]], 0)

    sections = [tall(s_ref[s], s) for s in range(6)]
    edges = [tall(e_ref[g], 6 + g) for g in range(2)]
    f32 = spectra(0, 0, sections, edges, c, w)
    scale = scales(0, sections, edges, c, w)
    store_scales(scale, w)
    f32_ref[...] = f32
    scale_ref[...] = scale
    maps(0, 9, f32, 0, c, w, o_ref)


def rest_kernel(z_ref, h_ref, f_ref, f32_ref, scale_ref, t_ref, _, o_ref, *scratch):
    c = Tables(t_ref)
    w = dict(zip((*SCRATCH, "f", "o", "sem"), scratch))
    flag = jnp.where(lax.axis_index("gz") == 0, 1.0, 0.0)
    w["f"][0] = f_ref[4]
    w["f"][1] = f_ref[5]
    tall = [
        jnp.concatenate([h_ref[16 * n : 16 * n + 16], z_ref[n], h_ref[48 + 16 * n : 64 + 16 * n]], 0)
        for n in range(3)
    ]
    extra = spectra(6, 2, tall[:2], tall[2:], c, w)
    scale = scales(6, tall[:2], tall[2:], c, w) * flag
    scale = jnp.where(lax.broadcasted_iota(jnp.int32, (32, 256), 0) % 8 >= 6, scale, scale_ref[...])
    store_scales(scale, w)
    f32 = jnp.where(lanes((128, 128)) % 32 >= 24, extra.astype(F32), f32_ref[...].astype(F32))
    maps(9, 12, f32, 4, c, w, o_ref)


def exchange(value_a, value_b, axis):
    sizes = [lax.axis_size(name) for name in AXES]
    along, across = AXES.index(axis), 1 - AXES.index(axis)

    def partner(place, first):
        place = list(place)
        up = place[along] % 2 == first
        moved = place[along] + (1 if up else -1)
        if 0 <= moved < sizes[along]:
            place[along] = moved
        else:
            place[across] ^= 1
        return place

    def pairs(first):
        return [
            (int(np.ravel_multi_index(at, sizes)), int(np.ravel_multi_index(partner(at, first), sizes)))
            for at in np.ndindex(*sizes)
        ]

    return lax.ppermute(value_a, AXES, pairs(0)), lax.ppermute(value_b, AXES, pairs(1))


def other(value):
    return lax.ppermute(value, "gz", [(0, 1), (1, 0)])


def shaped(*shape):
    return jax.ShapeDtypeStruct(shape, BF16)


def params(mib):
    return pltpu.CompilerParams(vmem_limit_bytes=mib * 2**20)


def compute(sections, edges, ya, yb, z, rows, table):
    scratch = [make(6) for make in SCRATCH.values()]
    out, f, f32, scale = pl.pallas_call(
        own_kernel,
        out_shape=(
            shaped(6, 2, 4, 128, 128),
            shaped(6, 4, 128, 128),
            shaped(128, 128),
            jax.ShapeDtypeStruct((32, 256), F32),
        ),
        in_specs=[VMEM] * 5,
        out_specs=(HBM, VMEM, VMEM, VMEM),
        scratch_shapes=scratch + [pltpu.VMEM((9, 4, 128, 128), BF16), pltpu.SemaphoreType.DMA((9,))],
        compiler_params=params(16),
        cost_estimate=pl.CostEstimate(flops=10**9, bytes_accessed=4 * 10**6, transcendentals=0),
    )(sections, edges, ya, yb, table)
    scratch = [make(2) for make in SCRATCH.values()]
    return pl.pallas_call(
        rest_kernel,
        out_shape=shaped(6, 2, 4, 128, 128),
        in_specs=[VMEM] * 6 + [HBM],
        out_specs=HBM,
        scratch_shapes=scratch
        + [
            pltpu.VMEM((4, 4, 128, 128), BF16),
            pltpu.VMEM((3, 4, 128, 128), BF16),
            pltpu.SemaphoreType.DMA((3,)),
        ],
        input_output_aliases={6: 0},
        compiler_params=params(16),
    )(z, rows, f, f32, scale, table, out)


def local(sections):
    edge = shaped(128, 128)
    fixed = [pltpu.with_memory_space_constraint(value, pltpu.HBM) for value in (sections, constants()[0])]
    xa, xb, sections, table = pl.pallas_call(
        edges_kernel,
        out_shape=(edge, edge, *(shaped(*value.shape) for value in fixed)),
        in_specs=[HBM] * 2,
        out_specs=(VMEM,) * 4,
        scratch_shapes=[pltpu.SemaphoreType.DMA((2,))],
        compiler_params=params(8),
    )(*fixed)
    xa, xb = exchange(xa, xb, "gx")
    edges, ya, yb, z = pl.pallas_call(
        rows_kernel,
        out_shape=(shaped(2, 128, 128), edge, edge, shaped(3, 128, 128)),
        in_specs=[VMEM] * 3,
        out_specs=(VMEM,) * 4,
        compiler_params=params(8),
    )(sections, xa, xb)
    ya, yb = exchange(ya, yb, "gy")
    z = other(z)
    rows = pl.pallas_call(
        halo_kernel,
        out_shape=shaped(96, 128),
        in_specs=[VMEM] * 2,
        out_specs=VMEM,
        compiler_params=params(8),
    )(ya, yb)
    rows = other(rows)
    out = compute(sections, edges, ya, yb, z, rows, table)
    out = out.reshape(6, 2, 4, 32, 4, 128).transpose(0, 1, 2, 4, 3, 5)
    return out.reshape(6, 2, 4, 4, 4096)


def solution(mesh):
    return jax.shard_map(
        local,
        mesh=mesh,
        in_specs=(P("gz", "gy", "gx"),),
        out_specs=P("gz", None, "gy", "gx", None),
        check_vma=False,
    )
```

```python
import functools
import math

import jax
import jax.numpy as jnp
import ml_dtypes
import numpy as np
from jax import lax
from jax.experimental import pallas as pl
from jax.experimental.pallas import tpu as pltpu
from jax.sharding import PartitionSpec as P

PATCH = 64
AXES = ("gx", "gy", "gz")
F32 = jnp.float32
BF16 = jnp.bfloat16
VMEM = pl.BlockSpec(memory_space=pltpu.VMEM)
HBM = pl.BlockSpec(memory_space=pltpu.HBM)


def rounded(values):
    return values.astype(np.float32).astype(ml_dtypes.bfloat16)


@functools.cache
def constants():
    index = np.arange(PATCH)
    angle = (index[:, None] * index[None, :] % PATCH) * (2.0 * math.pi / PATCH)
    cos = rounded(np.cos(angle)).astype(np.float64)
    sin = rounded(np.sin(angle)).astype(np.float64)
    sign = 1.0 - 2.0 * (index % 2)

    rows = np.zeros((160, 2, 4, 32))
    for j in range(4):
        rows[32 * j : 32 * j + 64, 0, j] = cos[:, :32]
        rows[32 * j : 32 * j + 64, 1, j] = -sin[:, :32]
        rows[32 * j : 32 * j + 64, 1, j, 0] = sign
    rows = rows.reshape(160, 256)

    forward = np.block([[cos, sin], [-sin, cos]])
    order = np.concatenate([index[0::2], index[1::2]])
    inverse = np.block([[cos[order], -sin[order]], [sin[order], cos[order]]])

    last = np.zeros((2, 4, 32, 4, 64))
    weight = np.where(index[:32] == 0, 1.0, 2.0)[:, None] / 4096.0
    for j in range(4):
        last[0, j, :, j] = weight * cos[:32]
        last[1, j, :, j] = -weight * sin[:32]
        last[1, j, 0, j] = sign / 4096.0
    even = last.reshape(256, 256)
    odd = last[:, :, :, [1, 0, 3, 2]].reshape(256, 256)

    column = np.full(256, -1000)
    column[:128] = np.arange(128) + 16
    column[128:144] = np.arange(16)
    column[192:208] = np.arange(16) + 144
    inside = np.stack([(column >= 32 * j) & (column < 32 * j + 64) for j in range(4)], 1)
    inside = inside.astype(np.float64)
    same_even = inside[:, [0, 2]] @ inside[:, [0, 2]].T
    same_odd = inside[:, [1, 3]] @ inside[:, [1, 3]].T
    spread = np.repeat(inside, 64, axis=1)
    lane_odd = (np.arange(256) // 64 % 2).astype(np.float64)
    means = np.concatenate([same_even, same_odd], 1)
    totals = np.concatenate([spread * (1 - lane_odd), spread * lane_odd], 0)
    tables = dict(
        own=rows[16:144],
        sides=np.concatenate([rows[:16], rows[144:]], 0),
        forward=forward,
        inverse=inverse,
        even=even,
        odd=odd,
        means=means,
        totals=totals,
    )
    pieces, places, at = [], {}, 0
    for name, table in tables.items():
        height, width = table.shape
        places[name] = (at, height, width // 128)
        pieces += np.split(table, width // 128, 1)
        at += height * width // 128
    return rounded(np.concatenate(pieces, 0)), places


class Tables:
    def __init__(self, ref):
        self.ref = ref

    def __getitem__(self, name):
        at, height, width = constants()[1][name]
        pieces = [self.ref[at + height * n : at + height * (n + 1)] for n in range(width)]
        return jnp.concatenate(pieces, 1) if width > 1 else pieces[0]


def dot(a, b):
    return jnp.dot(a, b, preferred_element_type=F32)


def dot_exact(a, ones):
    high = a.astype(BF16)
    rest = a - high.astype(F32)
    middle = rest.astype(BF16)
    low = (rest - middle.astype(F32)).astype(BF16)
    n = a.shape[0]
    parts = dot(jnp.concatenate([high, middle, low], 0), ones)
    return parts[2 * n :] + parts[n : 2 * n] + parts[:n]


def lanes(shape):
    return lax.broadcasted_iota(jnp.int32, shape, len(shape) - 1)


def first_kernel(s_hbm, a_ref, b_ref, sem):
    odd = lax.axis_index("gy") % 2 == 1
    copies = []
    for n, (out, at) in enumerate(((a_ref, jnp.where(odd, 0, 112)), (b_ref, jnp.where(odd, 112, 0)))):
        rows = s_hbm.at[:, pl.ds(pl.multiple_of(at, 16), 16), :]
        copies.append(pltpu.make_async_copy(rows, out, sem.at[n]))
    for copy in copies:
        copy.start()
    for copy in copies:
        copy.wait()


def pack_sides(blocks):
    lane = lanes(blocks[0].shape)
    left = jnp.zeros(lane.shape, F32)
    right = jnp.zeros(lane.shape, F32)
    for s, block in enumerate(blocks):
        block = block.astype(F32)
        here = (lane // 16) == s
        left = jnp.where(here, pltpu.roll(block, 16 * s, 1) if s else block, left)
        right = jnp.where(here, pltpu.roll(block, 16 * s + 16, 1), right)
    return left.astype(BF16), right.astype(BF16)


def stage_kernel(s_hbm, t_hbm, s_ref, t_ref, l_ref, r_ref, sem):
    sections = pltpu.make_async_copy(s_hbm, s_ref, sem.at[0])
    tables = pltpu.make_async_copy(t_hbm, t_ref, sem.at[1])
    sections.start()
    tables.start()
    sections.wait()
    l_ref[...], r_ref[...] = pack_sides([s_ref[s] for s in range(6)])
    tables.wait()


def sides_kernel(ya_ref, yb_ref, s_ref, l_ref, r_ref, _, a_ref, b_ref, z_ref):
    odd = lax.axis_index("gx") % 2 == 1
    top, bottom = low_high(ya_ref[...], yb_ref[...], "gy")
    left, right = pack_sides([jnp.concatenate([top[s], bottom[s]], 0) for s in range(6)])
    left = jnp.concatenate([left[:16], l_ref[...], left[16:]], 0)
    right = jnp.concatenate([right[:16], r_ref[...], right[16:]], 0)
    a_ref[...] = jnp.where(odd, left, right)
    b_ref[...] = jnp.where(odd, right, left)
    for s in range(2):
        z_ref[s] = jnp.concatenate([top[s], s_ref[s], bottom[s]], 0)


def side_tiles(xa_ref, xb_ref):
    left, right = low_high(xa_ref[...], xb_ref[...], "gx")
    left, right = left.astype(F32), right.astype(F32)
    low = lanes((160, 128)) < 64
    return jnp.where(low, left, pltpu.roll(right, 64, 1)), jnp.where(low, pltpu.roll(left, 64, 1), right)


def halo_kernel(xb_ref, xa_ref, h_ref):
    tile, _ = side_tiles(xa_ref, xb_ref)
    own = lanes((80, 128)) % 64 < 32
    h_ref[...] = jnp.where(own, tile[:80], pltpu.roll(tile[80:], 32, 1)).astype(BF16)


def low_high(a, b, axis):
    at = lax.axis_index(axis)
    odd = at % 2 == 1
    zero = jnp.zeros_like(a)
    low = jnp.where(odd, a, jnp.where(at == 0, zero, b))
    high = jnp.where(odd, jnp.where(at == lax.axis_size(axis) - 1, zero, b), a)
    return low, high


def column_stats(block):
    block = block.astype(F32).reshape(5, 32, 128)
    mean = jnp.sum(block, 1, keepdims=True) * (1.0 / 32)
    centred = block - mean
    return mean[:, 0], jnp.sum(centred * centred, 1)


def scales(first, sections, edges, c, w):
    edge_stats = [column_stats(g) for g in edges]
    w["mu"][...] = jnp.zeros(w["mu"].shape, F32)
    w["sq"][...] = jnp.zeros(w["sq"].shape, F32)
    for s, block in enumerate(sections):
        q, g = s % 4, s // 4
        mean, square = column_stats(block)
        mean_e, square_e = edge_stats[g]
        if q:
            mean_e = pltpu.roll(mean_e, 128 - 16 * q, 1)
            square_e = pltpu.roll(square_e, 128 - 16 * q, 1)
        w["mu"][:, first + s, :128] = mean
        w["mu"][:, first + s, 128:] = mean_e
        w["sq"][:, first + s, :128] = square
        w["sq"][:, first + s, 128:] = square_e
    mu = w["mu"][...]
    sq = w["sq"][...]
    mu0, mu1 = mu[:4].reshape(32, 256), mu[1:].reshape(32, 256)
    sq01 = (sq[:4] + sq[1:]).reshape(32, 256)
    sums = dot_exact(mu0 + mu1, c["means"])
    total = []
    for parity in range(2):
        centre = sums[:, 256 * parity : 256 * parity + 256] * (1.0 / 128)
        d0, d1 = mu0 - centre, mu1 - centre
        total.append(sq01 + 32.0 * (d0 * d0 + d1 * d1))
    variance = dot_exact(jnp.concatenate(total, 1), c["totals"]) * (1.0 / 4096)
    return lax.rsqrt(variance + 1e-05) * (1.0 / PATCH)


def store_scales(scale, w):
    for half in range(2):
        part = scale[:, 128 * half : 128 * half + 128]
        w["scale"][0, half] = part.reshape(4, 8, 128)
        w["scale"][1, half] = pltpu.roll(part, 64, 1).reshape(4, 8, 128)


def spectra(first, slot_f, sections, edges, c, w):
    lane = lanes((64, 128))
    zero_slot = lane % 32 == 0
    sides = c["sides"]
    for s, block in enumerate(sections):
        q = s % 4
        gap0 = jnp.zeros((16 * q, 256), BF16)
        gap1 = jnp.zeros((48 - 16 * q, 256), BF16)
        pieces = [c["own"], gap0, sides[:16], gap1, gap0, sides[16:], gap1]
        table = jnp.concatenate([p for p in pieces if p.shape[0]], 0)
        w["g"][s] = dot(jnp.concatenate([block, edges[s // 4]], 1), table)
    special = jnp.zeros((64, 128), F32)
    for s in range(len(sections)):
        for pair in range(2):
            columns = []
            for i in (2 * pair, 2 * pair + 1):
                re = w["g"][s, 32 * i : 32 * i + 64, :128]
                im = w["g"][s, 32 * i : 32 * i + 64, 128:]
                centre = jnp.sum(re, 0, keepdims=True) * (1.0 / 64)
                re = jnp.where(zero_slot, re - centre, re)
                slot = 4 * (s + first) + i
                special = jnp.where(lane % 32 == slot, pltpu.roll(im, slot, 1) if slot else im, special)
                im = jnp.where(zero_slot, 0.0, im)
                columns.append(jnp.concatenate([re, im], 0).astype(BF16))
            f = dot(c["forward"], jnp.concatenate(columns, 1)).astype(BF16)
            for n, i in enumerate((2 * pair, 2 * pair + 1)):
                w["f"][s + slot_f, i] = f[:, 128 * n : 128 * n + 128]
    return dot(c["forward"][:, :64], special.astype(BF16)).astype(BF16)


def maps(lo, hi, f32, offset, c, w, o_ref):
    lane = lanes((64, 128))
    zero_slot = lane % 32 == 0
    low = lanes((32, 128)) < 64
    f32 = f32.astype(F32)
    re, im = f32[:64], f32[64:]
    h32 = []
    for k in range(2):
        re_p = pltpu.roll(re, 128 - 4 * (k + 1), 1)
        im_p = pltpu.roll(im, 128 - 4 * (k + 1), 1)
        q = jnp.concatenate([re * re_p + im * im_p, im * re_p - re * im_p], 0).astype(BF16)
        h32.append(dot(c["inverse"][:64], q))

    def copy(p):
        return pltpu.make_async_copy(
            w["o"].at[p - lo], o_ref.at[p // 2, p % 2], w["sem"].at[p - lo]
        )

    def correlate(p):
        s, k = p // 2, p % 2
        spectra = []
        for half in range(2):
            columns = []
            for i in (2 * half, 2 * half + 1):
                here = w["f"][s - offset, i].astype(F32)
                there = w["f"][s + k + 1 - offset, i].astype(F32)
                f_re, f_im, p_re, p_im = here[:64], here[64:], there[:64], there[64:]
                q = jnp.concatenate([f_re * p_re + f_im * p_im, f_im * p_re - f_re * p_im], 0)
                columns.append(q.astype(BF16))
            spectra.append(dot(c["inverse"], jnp.concatenate(columns, 1)))
        return spectra

    def last(p, spectra):
        s, k = p // 2, p % 2
        even, odd = [], []
        for i in range(4):
            h = spectra[i // 2][:, 128 * (i % 2) : 128 * (i % 2) + 128]
            special = pltpu.roll(h32[k], (128 - 4 * s - i) % 128, 1)
            h_im = jnp.where(zero_slot, special, h[64:])
            h_cat = jnp.concatenate([h[:64], h_im], 1).astype(BF16)
            even.append(h_cat[:32])
            odd.append(h_cat[32:])
        even = dot(jnp.concatenate(even, 0), c["even"])
        odd = dot(jnp.concatenate(odd, 0), c["odd"])
        return even, odd

    def store(p, even, odd):
        s, k = p // 2, p % 2
        mix = w["mix"].at[p % 2]
        for i in range(4):
            for half in range(2):
                e_scale, o_scale = [
                    w["scale"][n, half, i, s : s + 1] * w["scale"][n, half, i, s + k + 1 : s + k + 2]
                    for n in range(2)
                ]
                e = even[32 * i : 32 * i + 32, 128 * half : 128 * half + 128] * e_scale
                o = odd[32 * i : 32 * i + 32, 128 * half : 128 * half + 128] * o_scale
                mix[i, pl.ds(2 * half, 32, stride=4), :] = jnp.where(low, e, o)
                mix[i, pl.ds(2 * half + 1, 32, stride=4), :] = pltpu.roll(jnp.where(low, o, e), 64, 1)
            w["o"][p - lo, i] = mix[i].astype(BF16)
        copy(p).start()

    ready = correlate(lo)
    for p in range(lo, hi):
        following = correlate(p + 1) if p + 1 < hi else None
        store(p, *last(p, ready))
        ready = following
    for p in range(lo, hi):
        copy(p).wait()


SCRATCH = dict(
    g=lambda n: pltpu.VMEM((n, 160, 256), F32),
    mu=lambda n: pltpu.VMEM((5, 8, 256), F32),
    sq=lambda n: pltpu.VMEM((5, 8, 256), F32),
    scale=lambda n: pltpu.VMEM((2, 2, 4, 8, 128), F32),
    mix=lambda n: pltpu.VMEM((2, 4, 128, 128), F32),
)


def own_kernel(xb_ref, xa_ref, ya_ref, yb_ref, s_ref, t_ref, o_ref, f_ref, f32_ref, scale_ref, *scratch):
    c = Tables(t_ref)
    w = dict(zip((*SCRATCH, "o", "sem"), scratch))
    w["f"] = f_ref
    top, bottom = low_high(ya_ref[...], yb_ref[...], "gy")
    sections = [jnp.concatenate([top[s], s_ref[s], bottom[s]], 0) for s in range(6)]
    edges = [tile.astype(BF16) for tile in side_tiles(xa_ref, xb_ref)]
    f32 = spectra(0, 0, sections, edges, c, w)
    scale = scales(0, sections, edges, c, w)
    store_scales(scale, w)
    f32_ref[...] = f32
    scale_ref[...] = scale
    maps(0, 9, f32, 0, c, w, o_ref)


def rest_kernel(z_ref, h_ref, f_ref, f32_ref, scale_ref, t_ref, _, o_ref, *scratch):
    c = Tables(t_ref)
    w = dict(zip((*SCRATCH, "f", "o", "sem"), scratch))
    flag = jnp.where(lax.axis_index("gz") == 0, 1.0, 0.0)
    w["f"][0] = f_ref[4]
    w["f"][1] = f_ref[5]
    sections = [z_ref[0], z_ref[1]]
    sides = h_ref[...]
    lower = pltpu.roll(sides.astype(F32), 96, 1).astype(BF16)
    edges = [jnp.concatenate([sides, lower], 0)]
    extra = spectra(6, 2, sections, edges, c, w)
    scale = scales(6, sections, edges, c, w) * flag
    scale = jnp.where(lax.broadcasted_iota(jnp.int32, (32, 256), 0) % 8 >= 6, scale, scale_ref[...])
    store_scales(scale, w)
    f32 = jnp.where(lanes((128, 128)) % 32 >= 24, extra.astype(F32), f32_ref[...].astype(F32))
    maps(9, 12, f32, 4, c, w, o_ref)


def exchange(value_a, value_b, axis):
    sizes = [lax.axis_size(name) for name in AXES]
    along, across = AXES.index(axis), 1 - AXES.index(axis)

    def partner(place, first):
        place = list(place)
        up = place[along] % 2 == first
        moved = place[along] + (1 if up else -1)
        if 0 <= moved < sizes[along]:
            place[along] = moved
        else:
            place[across] ^= 1
        return place

    def pairs(first):
        return [
            (int(np.ravel_multi_index(at, sizes)), int(np.ravel_multi_index(partner(at, first), sizes)))
            for at in np.ndindex(*sizes)
        ]

    value_b = lax.ppermute(value_b, AXES, pairs(1))
    return lax.ppermute(value_a, AXES, pairs(0)), value_b


def other(value):
    return lax.ppermute(value, "gz", [(0, 1), (1, 0)])


def shaped(*shape):
    return jax.ShapeDtypeStruct(shape, BF16)


def params(mib):
    return pltpu.CompilerParams(vmem_limit_bytes=mib * 2**20)


def compute(sections, xa, xb, ya, yb, z, sides, table):
    scratch = [make(6) for make in SCRATCH.values()]
    out, f, f32, scale = pl.pallas_call(
        own_kernel,
        out_shape=(
            shaped(6, 2, 4, 128, 128),
            shaped(6, 4, 128, 128),
            shaped(128, 128),
            jax.ShapeDtypeStruct((32, 256), F32),
        ),
        in_specs=[VMEM] * 6,
        out_specs=(HBM, VMEM, VMEM, VMEM),
        scratch_shapes=scratch + [pltpu.VMEM((9, 4, 128, 128), BF16), pltpu.SemaphoreType.DMA((9,))],
        compiler_params=params(16),
        cost_estimate=pl.CostEstimate(flops=10**9, bytes_accessed=4 * 10**6, transcendentals=0),
    )(xb, xa, ya, yb, sections, table)
    scratch = [make(2) for make in SCRATCH.values()]
    return pl.pallas_call(
        rest_kernel,
        out_shape=shaped(6, 2, 4, 128, 128),
        in_specs=[VMEM] * 6 + [HBM],
        out_specs=HBM,
        scratch_shapes=scratch
        + [
            pltpu.VMEM((4, 4, 128, 128), BF16),
            pltpu.VMEM((3, 4, 128, 128), BF16),
            pltpu.SemaphoreType.DMA((3,)),
        ],
        input_output_aliases={6: 0},
        compiler_params=params(16),
    )(z, sides, f, f32, scale, table, out)


def local(sections):
    pixels = pltpu.with_memory_space_constraint(sections, pltpu.HBM)
    table = constants()[0]
    rows, side, middle = shaped(6, 16, 128), shaped(160, 128), shaped(128, 128)
    ya, yb = pl.pallas_call(
        first_kernel,
        out_shape=(rows, rows),
        in_specs=[HBM],
        out_specs=(VMEM, VMEM),
        scratch_shapes=[pltpu.SemaphoreType.DMA((2,))],
        compiler_params=params(8),
    )(pixels)
    ya, yb = exchange(ya, yb, "gy")
    sections, table, left, right = pl.pallas_call(
        stage_kernel,
        out_shape=(shaped(*sections.shape), shaped(*table.shape), middle, middle),
        in_specs=[HBM, HBM],
        out_specs=(VMEM,) * 4,
        scratch_shapes=[pltpu.SemaphoreType.DMA((2,))],
        compiler_params=params(8),
        cost_estimate=pl.CostEstimate(flops=0, bytes_accessed=2 * 10**6, transcendentals=0),
    )(pixels, pltpu.with_memory_space_constraint(table, pltpu.HBM))
    xa, xb, z = pl.pallas_call(
        sides_kernel,
        out_shape=(side, side, shaped(2, 160, 128)),
        in_specs=[VMEM] * 6,
        out_specs=(VMEM,) * 3,
        compiler_params=params(8),
    )(ya, yb, sections, left, right, table)
    xa, xb = exchange(xa, xb, "gx")
    z = other(z)
    sides = pl.pallas_call(
        halo_kernel,
        out_shape=shaped(80, 128),
        in_specs=[VMEM] * 2,
        out_specs=VMEM,
        compiler_params=params(8),
    )(xb, xa)
    sides = other(sides)
    out = compute(sections, xa, xb, ya, yb, z, sides, table)
    out = out.reshape(6, 2, 4, 32, 4, 128).transpose(0, 1, 2, 4, 3, 5)
    return out.reshape(6, 2, 4, 4, 4096)


def solution(mesh):
    return jax.shard_map(
        local,
        mesh=mesh,
        in_specs=(P("gz", "gy", "gx"),),
        out_specs=P("gz", None, "gy", "gx", None),
        check_vma=False,
    )
```

```python
import functools
import math

import jax
import jax.numpy as jnp
import ml_dtypes
import numpy as np
from jax import lax
from jax.experimental import pallas as pl
from jax.experimental.pallas import tpu as pltpu
from jax.sharding import PartitionSpec as P

PATCH = 64
AXES = ("gx", "gy", "gz")
F32 = jnp.float32
BF16 = jnp.bfloat16
VMEM = pl.BlockSpec(memory_space=pltpu.VMEM)
HBM = pl.BlockSpec(memory_space=pltpu.HBM)


def rounded(values):
    return values.astype(np.float32).astype(ml_dtypes.bfloat16)


@functools.cache
def constants():
    index = np.arange(PATCH)
    angle = (index[:, None] * index[None, :] % PATCH) * (2.0 * math.pi / PATCH)
    cos = rounded(np.cos(angle)).astype(np.float64)
    sin = rounded(np.sin(angle)).astype(np.float64)
    sign = 1.0 - 2.0 * (index % 2)

    rows = np.zeros((160, 2, 4, 32))
    for j in range(4):
        rows[32 * j : 32 * j + 64, 0, j] = cos[:, :32]
        rows[32 * j : 32 * j + 64, 1, j] = -sin[:, :32]
        rows[32 * j : 32 * j + 64, 1, j, 0] = sign
    rows = rows.reshape(160, 256)

    forward = np.block([[cos, sin], [-sin, cos]])
    order = np.concatenate([index[0::2], index[1::2]])
    inverse = np.block([[cos[order], -sin[order]], [sin[order], cos[order]]])

    last = np.zeros((2, 4, 32, 4, 64))
    weight = np.where(index[:32] == 0, 1.0, 2.0)[:, None] / 4096.0
    for j in range(4):
        last[0, j, :, j] = weight * cos[:32]
        last[1, j, :, j] = -weight * sin[:32]
        last[1, j, 0, j] = sign / 4096.0
    even = last.reshape(256, 256)
    odd = last[:, :, :, [1, 0, 3, 2]].reshape(256, 256)

    column = np.full(256, -1000)
    column[:128] = np.arange(128) + 16
    column[128:144] = np.arange(16)
    column[192:208] = np.arange(16) + 144
    inside = np.stack([(column >= 32 * j) & (column < 32 * j + 64) for j in range(4)], 1)
    inside = inside.astype(np.float64)
    same_even = inside[:, [0, 2]] @ inside[:, [0, 2]].T
    same_odd = inside[:, [1, 3]] @ inside[:, [1, 3]].T
    spread = np.repeat(inside, 64, axis=1)
    lane_odd = (np.arange(256) // 64 % 2).astype(np.float64)
    means = np.concatenate([same_even, same_odd], 1)
    totals = np.concatenate([spread * (1 - lane_odd), spread * lane_odd], 0)
    tables = dict(
        own=rows[16:144],
        sides=np.concatenate([rows[:16], rows[144:]], 0),
        forward=forward,
        inverse=inverse,
        even=even,
        odd=odd,
        means=means,
        totals=totals,
    )
    pieces, places, at = [], {}, 0
    for name, table in tables.items():
        height, width = table.shape
        places[name] = (at, height, width // 128)
        pieces += np.split(table, width // 128, 1)
        at += height * width // 128
    return rounded(np.concatenate(pieces, 0)), places


class Tables:
    def __init__(self, ref):
        self.ref = ref

    def __getitem__(self, name):
        at, height, width = constants()[1][name]
        pieces = [self.ref[at + height * n : at + height * (n + 1)] for n in range(width)]
        return jnp.concatenate(pieces, 1) if width > 1 else pieces[0]


def dot(a, b):
    return jnp.dot(a, b, preferred_element_type=F32)


def dot_exact(a, ones):
    high = a.astype(BF16)
    rest = a - high.astype(F32)
    middle = rest.astype(BF16)
    low = (rest - middle.astype(F32)).astype(BF16)
    n = a.shape[0]
    parts = dot(jnp.concatenate([high, middle, low], 0), ones)
    return parts[2 * n :] + parts[n : 2 * n] + parts[:n]


def lanes(shape):
    return lax.broadcasted_iota(jnp.int32, shape, len(shape) - 1)


def first_kernel(s_hbm, a_ref, b_ref, sem):
    odd = lax.axis_index("gy") % 2 == 1
    copies = []
    for n, (out, at) in enumerate(((a_ref, jnp.where(odd, 0, 112)), (b_ref, jnp.where(odd, 112, 0)))):
        rows = s_hbm.at[:, pl.ds(pl.multiple_of(at, 16), 16), :]
        copies.append(pltpu.make_async_copy(rows, out, sem.at[n]))
    for copy in copies:
        copy.start()
    for copy in copies:
        copy.wait()


def pack_sides(blocks):
    lane = lanes(blocks[0].shape)
    left = jnp.zeros(lane.shape, F32)
    right = jnp.zeros(lane.shape, F32)
    for s, block in enumerate(blocks):
        block = block.astype(F32)
        left = jnp.where(lane // 16 == (s + 4) % 8, pltpu.roll(block, (16 * s + 64) % 128, 1) if s != 4 else block, left)
        right = jnp.where(lane // 16 == s, pltpu.roll(block, 16 * s + 16, 1), right)
    return left.astype(BF16), right.astype(BF16)


def stage_kernel(s_hbm, t_hbm, s_ref, t_ref, l_ref, r_ref, sem):
    sections = pltpu.make_async_copy(s_hbm, s_ref, sem.at[0])
    tables = pltpu.make_async_copy(t_hbm, t_ref, sem.at[1])
    sections.start()
    tables.start()
    sections.wait()
    l_ref[...], r_ref[...] = pack_sides([s_ref[s] for s in range(6)])
    tables.wait()


def sides_kernel(ya_ref, yb_ref, s_ref, l_ref, r_ref, _, a_ref, b_ref, z_ref):
    odd = lax.axis_index("gx") % 2 == 1
    top, bottom = low_high(ya_ref[...], yb_ref[...], "gy")
    left, right = pack_sides([jnp.concatenate([top[s], bottom[s]], 0) for s in range(6)])
    left = jnp.concatenate([left[:16], l_ref[...], left[16:]], 0)
    right = jnp.concatenate([right[:16], r_ref[...], right[16:]], 0)
    a_ref[...] = jnp.where(odd, left, right)
    b_ref[...] = jnp.where(odd, right, left)
    for s in range(2):
        z_ref[s] = jnp.concatenate([top[s], s_ref[s], bottom[s]], 0)


def side_tiles(xa_ref, xb_ref):
    left, right = low_high(xa_ref[...], xb_ref[...], "gx")
    low = lanes((160, 128)) < 64
    return jnp.where(low, left, right), jnp.where(low, right, left)


def halo_kernel(xb_ref, xa_ref, h_ref):
    tile = side_tiles(xa_ref, xb_ref)[0].astype(F32)
    own = lanes((80, 128)) % 64 < 32
    h_ref[...] = jnp.where(own, tile[:80], pltpu.roll(tile[80:], 32, 1)).astype(BF16)


def low_high(a, b, axis):
    at = lax.axis_index(axis)
    odd = at % 2 == 1
    zero = jnp.zeros_like(a)
    low = jnp.where(odd, a, jnp.where(at == 0, zero, b))
    high = jnp.where(odd, jnp.where(at == lax.axis_size(axis) - 1, zero, b), a)
    return low, high


def column_stats(block):
    block = block.astype(F32).reshape(5, 32, 128)
    mean = jnp.sum(block, 1, keepdims=True) * (1.0 / 32)
    centred = block - mean
    return mean[:, 0], jnp.sum(centred * centred, 1)


def scales(first, sections, edges, c, w):
    edge_stats = [column_stats(g) for g in edges]
    w["mu"][...] = jnp.zeros(w["mu"].shape, F32)
    w["sq"][...] = jnp.zeros(w["sq"].shape, F32)
    for s, block in enumerate(sections):
        q, g = s % 4, s // 4
        mean, square = column_stats(block)
        mean_e, square_e = edge_stats[g]
        if s:
            mean_e = pltpu.roll(mean_e, 128 - 16 * q - 64 * g, 1)
            square_e = pltpu.roll(square_e, 128 - 16 * q - 64 * g, 1)
        w["mu"][:, first + s, :128] = mean
        w["mu"][:, first + s, 128:] = mean_e
        w["sq"][:, first + s, :128] = square
        w["sq"][:, first + s, 128:] = square_e
    mu = w["mu"][...]
    sq = w["sq"][...]
    mu0, mu1 = mu[:4].reshape(32, 256), mu[1:].reshape(32, 256)
    sq01 = (sq[:4] + sq[1:]).reshape(32, 256)
    sums = dot_exact(mu0 + mu1, c["means"])
    total = []
    for parity in range(2):
        centre = sums[:, 256 * parity : 256 * parity + 256] * (1.0 / 128)
        d0, d1 = mu0 - centre, mu1 - centre
        total.append(sq01 + 32.0 * (d0 * d0 + d1 * d1))
    variance = dot_exact(jnp.concatenate(total, 1), c["totals"]) * (1.0 / 4096)
    return lax.rsqrt(variance + 1e-05) * (1.0 / PATCH)


def store_scales(scale, w):
    for half in range(2):
        part = scale[:, 128 * half : 128 * half + 128]
        w["scale"][0, half] = part.reshape(4, 8, 128)
        w["scale"][1, half] = pltpu.roll(part, 64, 1).reshape(4, 8, 128)


def spectra(first, slot_f, sections, edges, c, w):
    lane = lanes((64, 128))
    zero_slot = lane % 32 == 0
    sides = c["sides"]
    for s, block in enumerate(sections):
        q = s % 4
        gap0 = jnp.zeros((16 * q, 256), BF16)
        gap1 = jnp.zeros((48 - 16 * q, 256), BF16)
        one, two = (sides[:16], sides[16:]) if s < 4 else (sides[16:], sides[:16])
        pieces = [c["own"], gap0, one, gap1, gap0, two, gap1]
        table = jnp.concatenate([p for p in pieces if p.shape[0]], 0)
        w["g"][s] = dot(jnp.concatenate([block, edges[s // 4]], 1), table)
    special = jnp.zeros((64, 128), F32)
    for s in range(len(sections)):
        for pair in range(2):
            columns = []
            for i in (2 * pair, 2 * pair + 1):
                re = w["g"][s, 32 * i : 32 * i + 64, :128]
                im = w["g"][s, 32 * i : 32 * i + 64, 128:]
                centre = jnp.sum(re, 0, keepdims=True) * (1.0 / 64)
                re = jnp.where(zero_slot, re - centre, re)
                slot = 4 * (s + first) + i
                special = jnp.where(lane % 32 == slot, pltpu.roll(im, slot, 1) if slot else im, special)
                im = jnp.where(zero_slot, 0.0, im)
                columns.append(jnp.concatenate([re, im], 0).astype(BF16))
            f = dot(c["forward"], jnp.concatenate(columns, 1)).astype(BF16)
            for n, i in enumerate((2 * pair, 2 * pair + 1)):
                w["f"][s + slot_f, i] = f[:, 128 * n : 128 * n + 128]
    return dot(c["forward"][:, :64], special.astype(BF16)).astype(BF16)


def maps(lo, hi, f32, offset, c, w, o_ref):
    lane = lanes((64, 128))
    zero_slot = lane % 32 == 0
    low = lanes((32, 128)) < 64
    f32 = f32.astype(F32)
    re, im = f32[:64], f32[64:]
    h32 = []
    for k in range(2):
        re_p = pltpu.roll(re, 128 - 4 * (k + 1), 1)
        im_p = pltpu.roll(im, 128 - 4 * (k + 1), 1)
        q = jnp.concatenate([re * re_p + im * im_p, im * re_p - re * im_p], 0).astype(BF16)
        h32.append(dot(c["inverse"][:64], q))

    def copy(p):
        return pltpu.make_async_copy(
            w["o"].at[p - lo], o_ref.at[p // 2, p % 2], w["sem"].at[p - lo]
        )

    def correlate(p):
        s, k = p // 2, p % 2
        spectra = []
        for half in range(2):
            columns = []
            for i in (2 * half, 2 * half + 1):
                here = w["f"][s - offset, i].astype(F32)
                there = w["f"][s + k + 1 - offset, i].astype(F32)
                f_re, f_im, p_re, p_im = here[:64], here[64:], there[:64], there[64:]
                q = jnp.concatenate([f_re * p_re + f_im * p_im, f_im * p_re - f_re * p_im], 0)
                columns.append(q.astype(BF16))
            spectra.append(dot(c["inverse"], jnp.concatenate(columns, 1)))
        return spectra

    def last(p, spectra):
        s, k = p // 2, p % 2
        even, odd = [], []
        for i in range(4):
            h = spectra[i // 2][:, 128 * (i % 2) : 128 * (i % 2) + 128]
            special = pltpu.roll(h32[k], (128 - 4 * s - i) % 128, 1)
            h_im = jnp.where(zero_slot, special, h[64:])
            h_cat = jnp.concatenate([h[:64], h_im], 1).astype(BF16)
            even.append(h_cat[:32])
            odd.append(h_cat[32:])
        even = dot(jnp.concatenate(even, 0), c["even"])
        odd = dot(jnp.concatenate(odd, 0), c["odd"])
        return even, odd

    def store(p, even, odd):
        s, k = p // 2, p % 2
        mix = w["mix"].at[p % 2]
        for i in range(4):
            for half in range(2):
                e_scale, o_scale = [
                    w["scale"][n, half, i, s : s + 1] * w["scale"][n, half, i, s + k + 1 : s + k + 2]
                    for n in range(2)
                ]
                e = even[32 * i : 32 * i + 32, 128 * half : 128 * half + 128] * e_scale
                o = odd[32 * i : 32 * i + 32, 128 * half : 128 * half + 128] * o_scale
                mix[i, pl.ds(2 * half, 32, stride=4), :] = jnp.where(low, e, o)
                mix[i, pl.ds(2 * half + 1, 32, stride=4), :] = pltpu.roll(jnp.where(low, o, e), 64, 1)
            w["o"][p - lo, i] = mix[i].astype(BF16)
        copy(p).start()

    ready = {}
    for p in range(lo, hi + 2):
        if p < hi:
            ready[p] = correlate(p)
        if p >= lo + 2:
            store(p - 2, *last(p - 2, ready.pop(p - 2)))
    for p in range(lo, hi):
        copy(p).wait()


SCRATCH = dict(
    g=lambda n: pltpu.VMEM((n, 160, 256), F32),
    mu=lambda n: pltpu.VMEM((5, 8, 256), F32),
    sq=lambda n: pltpu.VMEM((5, 8, 256), F32),
    scale=lambda n: pltpu.VMEM((2, 2, 4, 8, 128), F32),
    mix=lambda n: pltpu.VMEM((2, 4, 128, 128), F32),
)


def own_kernel(xb_ref, xa_ref, ya_ref, yb_ref, s_ref, t_ref, o_ref, f_ref, f32_ref, scale_ref, *scratch):
    c = Tables(t_ref)
    w = dict(zip((*SCRATCH, "o", "sem"), scratch))
    w["f"] = f_ref
    top, bottom = low_high(ya_ref[...], yb_ref[...], "gy")
    sections = [jnp.concatenate([top[s], s_ref[s], bottom[s]], 0) for s in range(6)]
    edges = side_tiles(xa_ref, xb_ref)
    f32 = spectra(0, 0, sections, edges, c, w)
    scale = scales(0, sections, edges, c, w)
    store_scales(scale, w)
    f32_ref[...] = f32
    scale_ref[...] = scale
    maps(0, 9, f32, 0, c, w, o_ref)


def rest_kernel(z_ref, h_ref, f_ref, f32_ref, scale_ref, t_ref, _, o_ref, *scratch):
    c = Tables(t_ref)
    w = dict(zip((*SCRATCH, "f", "o", "sem"), scratch))
    flag = jnp.where(lax.axis_index("gz") == 0, 1.0, 0.0)
    w["f"][0] = f_ref[4]
    w["f"][1] = f_ref[5]
    sections = [z_ref[0], z_ref[1]]
    sides = h_ref[...]
    lower = pltpu.roll(sides.astype(F32), 96, 1).astype(BF16)
    edges = [jnp.concatenate([sides, lower], 0)]
    extra = spectra(6, 2, sections, edges, c, w)
    scale = scales(6, sections, edges, c, w) * flag
    scale = jnp.where(lax.broadcasted_iota(jnp.int32, (32, 256), 0) % 8 >= 6, scale, scale_ref[...])
    store_scales(scale, w)
    f32 = jnp.where(lanes((128, 128)) % 32 >= 24, extra.astype(F32), f32_ref[...].astype(F32))
    maps(9, 12, f32, 4, c, w, o_ref)


def exchange(value_a, value_b, axis):
    sizes = [lax.axis_size(name) for name in AXES]
    along, across = AXES.index(axis), 1 - AXES.index(axis)

    def partner(place, first):
        place = list(place)
        up = place[along] % 2 == first
        moved = place[along] + (1 if up else -1)
        if 0 <= moved < sizes[along]:
            place[along] = moved
        else:
            place[across] ^= 1
        return place

    def pairs(first):
        return [
            (int(np.ravel_multi_index(at, sizes)), int(np.ravel_multi_index(partner(at, first), sizes)))
            for at in np.ndindex(*sizes)
        ]

    value_b = lax.ppermute(value_b, AXES, pairs(1))
    return lax.ppermute(value_a, AXES, pairs(0)), value_b


def other(value):
    return lax.ppermute(value, "gz", [(0, 1), (1, 0)])


def shaped(*shape):
    return jax.ShapeDtypeStruct(shape, BF16)


def params(mib):
    return pltpu.CompilerParams(vmem_limit_bytes=mib * 2**20)


def compute(sections, xa, xb, ya, yb, z, sides, table):
    scratch = [make(6) for make in SCRATCH.values()]
    out, f, f32, scale = pl.pallas_call(
        own_kernel,
        out_shape=(
            shaped(6, 2, 4, 128, 128),
            shaped(6, 4, 128, 128),
            shaped(128, 128),
            jax.ShapeDtypeStruct((32, 256), F32),
        ),
        in_specs=[VMEM] * 6,
        out_specs=(HBM, VMEM, VMEM, VMEM),
        scratch_shapes=scratch + [pltpu.VMEM((9, 4, 128, 128), BF16), pltpu.SemaphoreType.DMA((9,))],
        compiler_params=params(16),
        cost_estimate=pl.CostEstimate(flops=10**9, bytes_accessed=4 * 10**6, transcendentals=0),
    )(xb, xa, ya, yb, sections, table)
    scratch = [make(2) for make in SCRATCH.values()]
    return pl.pallas_call(
        rest_kernel,
        out_shape=shaped(6, 2, 4, 128, 128),
        in_specs=[VMEM] * 6 + [HBM],
        out_specs=HBM,
        scratch_shapes=scratch
        + [
            pltpu.VMEM((4, 4, 128, 128), BF16),
            pltpu.VMEM((3, 4, 128, 128), BF16),
            pltpu.SemaphoreType.DMA((3,)),
        ],
        input_output_aliases={6: 0},
        compiler_params=params(16),
    )(z, sides, f, f32, scale, table, out)


def local(sections):
    pixels = pltpu.with_memory_space_constraint(sections, pltpu.HBM)
    table = constants()[0]
    rows, side, middle = shaped(6, 16, 128), shaped(160, 128), shaped(128, 128)
    ya, yb = pl.pallas_call(
        first_kernel,
        out_shape=(rows, rows),
        in_specs=[HBM],
        out_specs=(VMEM, VMEM),
        scratch_shapes=[pltpu.SemaphoreType.DMA((2,))],
        compiler_params=params(8),
    )(pixels)
    ya, yb = exchange(ya, yb, "gy")
    sections, table, left, right = pl.pallas_call(
        stage_kernel,
        out_shape=(shaped(*sections.shape), shaped(*table.shape), middle, middle),
        in_specs=[HBM, HBM],
        out_specs=(VMEM,) * 4,
        scratch_shapes=[pltpu.SemaphoreType.DMA((2,))],
        compiler_params=params(8),
        cost_estimate=pl.CostEstimate(flops=0, bytes_accessed=2 * 10**6, transcendentals=0),
    )(pixels, pltpu.with_memory_space_constraint(table, pltpu.HBM))
    xa, xb, z = pl.pallas_call(
        sides_kernel,
        out_shape=(side, side, shaped(2, 160, 128)),
        in_specs=[VMEM] * 6,
        out_specs=(VMEM,) * 3,
        compiler_params=params(8),
    )(ya, yb, sections, left, right, table)
    xa, xb = exchange(xa, xb, "gx")
    z = other(z)
    sides = pl.pallas_call(
        halo_kernel,
        out_shape=shaped(80, 128),
        in_specs=[VMEM] * 2,
        out_specs=VMEM,
        compiler_params=params(8),
    )(xb, xa)
    sides = other(sides)
    out = compute(sections, xa, xb, ya, yb, z, sides, table)
    out = out.reshape(6, 2, 4, 32, 4, 128).transpose(0, 1, 2, 4, 3, 5)
    return out.reshape(6, 2, 4, 4, 4096)


def solution(mesh):
    return jax.shard_map(
        local,
        mesh=mesh,
        in_specs=(P("gz", "gy", "gx"),),
        out_specs=P("gz", None, "gy", "gx", None),
        check_vma=False,
    )
```

```python
import functools
import math

import jax
import jax.numpy as jnp
import ml_dtypes
import numpy as np
from jax import lax
from jax.experimental import pallas as pl
from jax.experimental.pallas import tpu as pltpu
from jax.sharding import PartitionSpec as P

PATCH = 64
AXES = ("gx", "gy", "gz")
F32 = jnp.float32
BF16 = jnp.bfloat16
VMEM = pl.BlockSpec(memory_space=pltpu.VMEM)
HBM = pl.BlockSpec(memory_space=pltpu.HBM)


def rounded(values):
    return values.astype(np.float32).astype(ml_dtypes.bfloat16)


@functools.cache
def constants():
    index = np.arange(PATCH)
    angle = (index[:, None] * index[None, :] % PATCH) * (2.0 * math.pi / PATCH)
    cos = rounded(np.cos(angle)).astype(np.float64)
    sin = rounded(np.sin(angle)).astype(np.float64)
    sign = 1.0 - 2.0 * (index % 2)

    rows = np.zeros((160, 2, 4, 32))
    for j in range(4):
        rows[32 * j : 32 * j + 64, 0, j] = cos[:, :32]
        rows[32 * j : 32 * j + 64, 1, j] = -sin[:, :32]
        rows[32 * j : 32 * j + 64, 1, j, 0] = sign
    rows = rows.reshape(160, 256)

    forward = np.block([[cos, sin], [-sin, cos]])
    order = np.concatenate([index[0::2], index[1::2]])
    inverse = np.block([[cos[order], -sin[order]], [sin[order], cos[order]]])

    last = np.zeros((2, 4, 32, 4, 64))
    weight = np.where(index[:32] == 0, 1.0, 2.0)[:, None] / 4096.0
    for j in range(4):
        last[0, j, :, j] = weight * cos[:32]
        last[1, j, :, j] = -weight * sin[:32]
        last[1, j, 0, j] = sign / 4096.0
    even = last.reshape(256, 256)
    odd = last[:, :, :, [1, 0, 3, 2]].reshape(256, 256)

    column = np.full(256, -1000)
    column[:128] = np.arange(128) + 16
    column[128:144] = np.arange(16)
    column[192:208] = np.arange(16) + 144
    inside = np.stack([(column >= 32 * j) & (column < 32 * j + 64) for j in range(4)], 1)
    inside = inside.astype(np.float64)
    same_even = inside[:, [0, 2]] @ inside[:, [0, 2]].T
    same_odd = inside[:, [1, 3]] @ inside[:, [1, 3]].T
    spread = np.repeat(inside, 64, axis=1)
    lane_odd = (np.arange(256) // 64 % 2).astype(np.float64)
    means = np.concatenate([same_even, same_odd], 1)
    totals = np.concatenate([spread * (1 - lane_odd), spread * lane_odd], 0)
    tables = dict(
        own=rows[16:144],
        sides=np.concatenate([rows[:16], rows[144:]], 0),
        forward=forward,
        inverse=inverse,
        even=even,
        odd=odd,
        means=means,
        totals=totals,
    )
    pieces, places, at = [], {}, 0
    for name, table in tables.items():
        height, width = table.shape
        places[name] = (at, height, width // 128)
        pieces += np.split(table, width // 128, 1)
        at += height * width // 128
    return rounded(np.concatenate(pieces, 0)), places


class Tables:
    def __init__(self, ref):
        self.ref = ref

    def __getitem__(self, name):
        at, height, width = constants()[1][name]
        pieces = [self.ref[at + height * n : at + height * (n + 1)] for n in range(width)]
        return jnp.concatenate(pieces, 1) if width > 1 else pieces[0]


def dot(a, b):
    return jnp.dot(a, b, preferred_element_type=F32)


def dot_exact(a, ones):
    high = a.astype(BF16)
    rest = a - high.astype(F32)
    middle = rest.astype(BF16)
    low = (rest - middle.astype(F32)).astype(BF16)
    n = a.shape[0]
    parts = dot(jnp.concatenate([high, middle, low], 0), ones)
    return parts[2 * n :] + parts[n : 2 * n] + parts[:n]


def lanes(shape):
    return lax.broadcasted_iota(jnp.int32, shape, len(shape) - 1)


def first_kernel(s_hbm, a_ref, b_ref, sem):
    odd = lax.axis_index("gy") % 2 == 1
    copies = []
    for n, (out, at) in enumerate(((a_ref, jnp.where(odd, 0, 112)), (b_ref, jnp.where(odd, 112, 0)))):
        rows = s_hbm.at[:, pl.ds(pl.multiple_of(at, 16), 16), :]
        copies.append(pltpu.make_async_copy(rows, out, sem.at[n]))
    for copy in copies:
        copy.start()
    for copy in copies:
        copy.wait()


def pack_sides(blocks):
    lane = lanes(blocks[0].shape)
    left = jnp.zeros(lane.shape, F32)
    right = jnp.zeros(lane.shape, F32)
    for s, block in enumerate(blocks):
        block = block.astype(F32)
        left = jnp.where(lane // 16 == (s + 4) % 8, pltpu.roll(block, (16 * s + 64) % 128, 1) if s != 4 else block, left)
        right = jnp.where(lane // 16 == s, pltpu.roll(block, 16 * s + 16, 1), right)
    return left.astype(BF16), right.astype(BF16)


def stage_kernel(s_hbm, t_hbm, s_ref, t_ref, l_ref, r_ref, sem):
    sections = pltpu.make_async_copy(s_hbm, s_ref, sem.at[0])
    tables = pltpu.make_async_copy(t_hbm, t_ref, sem.at[1])
    sections.start()
    tables.start()
    sections.wait()
    l_ref[...], r_ref[...] = pack_sides([s_ref[s] for s in range(6)])
    tables.wait()


def sides_kernel(ya_ref, yb_ref, s_ref, l_ref, r_ref, _, a_ref, b_ref, z_ref):
    odd = lax.axis_index("gx") % 2 == 1
    top, bottom = low_high(ya_ref[...], yb_ref[...], "gy")
    left, right = pack_sides([jnp.concatenate([top[s], bottom[s]], 0) for s in range(6)])
    left = jnp.concatenate([left[:16], l_ref[...], left[16:]], 0)
    right = jnp.concatenate([right[:16], r_ref[...], right[16:]], 0)
    a_ref[...] = jnp.where(odd, left, right)
    b_ref[...] = jnp.where(odd, right, left)
    for s in range(2):
        z_ref[s] = jnp.concatenate([top[s], s_ref[s], bottom[s]], 0)


def side_tiles(xa_ref, xb_ref):
    left, right = low_high(xa_ref[...], xb_ref[...], "gx")
    low = lanes((160, 128)) < 64
    return jnp.where(low, left, right), jnp.where(low, right, left)


def halo_kernel(xb_ref, xa_ref, h_ref):
    tile = side_tiles(xa_ref, xb_ref)[0].astype(F32)
    own = lanes((80, 128)) % 64 < 32
    h_ref[...] = jnp.where(own, tile[:80], pltpu.roll(tile[80:], 32, 1)).astype(BF16)


def low_high(a, b, axis):
    at = lax.axis_index(axis)
    odd = at % 2 == 1
    zero = jnp.zeros_like(a)
    low = jnp.where(odd, a, jnp.where(at == 0, zero, b))
    high = jnp.where(odd, jnp.where(at == lax.axis_size(axis) - 1, zero, b), a)
    return low, high


def column_stats(block):
    block = block.astype(F32).reshape(5, 32, 128)
    mean = jnp.sum(block, 1, keepdims=True) * (1.0 / 32)
    centred = block - mean
    return mean[:, 0], jnp.sum(centred * centred, 1)


def scales(first, sections, edges, c, w):
    edge_stats = [column_stats(g) for g in edges]
    w["mu"][...] = jnp.zeros(w["mu"].shape, F32)
    w["sq"][...] = jnp.zeros(w["sq"].shape, F32)
    for s, block in enumerate(sections):
        q, g = s % 4, s // 4
        mean, square = column_stats(block)
        mean_e, square_e = edge_stats[g]
        if s:
            mean_e = pltpu.roll(mean_e, 128 - 16 * q - 64 * g, 1)
            square_e = pltpu.roll(square_e, 128 - 16 * q - 64 * g, 1)
        w["mu"][:, first + s, :128] = mean
        w["mu"][:, first + s, 128:] = mean_e
        w["sq"][:, first + s, :128] = square
        w["sq"][:, first + s, 128:] = square_e
    mu = w["mu"][...]
    sq = w["sq"][...]
    mu0, mu1 = mu[:4].reshape(32, 256), mu[1:].reshape(32, 256)
    sq01 = (sq[:4] + sq[1:]).reshape(32, 256)
    sums = dot_exact(mu0 + mu1, c["means"])
    total = []
    for parity in range(2):
        centre = sums[:, 256 * parity : 256 * parity + 256] * (1.0 / 128)
        d0, d1 = mu0 - centre, mu1 - centre
        total.append(sq01 + 32.0 * (d0 * d0 + d1 * d1))
    variance = dot_exact(jnp.concatenate(total, 1), c["totals"]) * (1.0 / 4096)
    return lax.rsqrt(variance + 1e-05) * (1.0 / PATCH)


def store_scales(scale, w):
    for half in range(2):
        part = scale[:, 128 * half : 128 * half + 128]
        w["scale"][0, half] = part.reshape(4, 8, 128)
        w["scale"][1, half] = pltpu.roll(part, 64, 1).reshape(4, 8, 128)


def spectra(first, slot_f, sections, edges, c, w):
    lane = lanes((64, 128))
    zero_slot = lane % 32 == 0
    sides = c["sides"]
    for s, block in enumerate(sections):
        q = s % 4
        gap0 = jnp.zeros((16 * q, 256), BF16)
        gap1 = jnp.zeros((48 - 16 * q, 256), BF16)
        one, two = (sides[:16], sides[16:]) if s < 4 else (sides[16:], sides[:16])
        pieces = [c["own"], gap0, one, gap1, gap0, two, gap1]
        table = jnp.concatenate([p for p in pieces if p.shape[0]], 0)
        w["g"][s] = dot(jnp.concatenate([block, edges[s // 4]], 1), table)
    special = jnp.zeros((64, 128), F32)
    for s in range(len(sections)):
        for pair in range(2):
            columns = []
            for i in (2 * pair, 2 * pair + 1):
                re = w["g"][s, 32 * i : 32 * i + 64, :128]
                im = w["g"][s, 32 * i : 32 * i + 64, 128:]
                centre = jnp.sum(re, 0, keepdims=True) * (1.0 / 64)
                re = jnp.where(zero_slot, re - centre, re)
                slot = 4 * (s + first) + i
                special = jnp.where(lane % 32 == slot, pltpu.roll(im, slot, 1) if slot else im, special)
                im = jnp.where(zero_slot, 0.0, im)
                columns.append(jnp.concatenate([re, im], 0).astype(BF16))
            f = dot(c["forward"], jnp.concatenate(columns, 1)).astype(BF16)
            for n, i in enumerate((2 * pair, 2 * pair + 1)):
                w["f"][s + slot_f, i] = f[:, 128 * n : 128 * n + 128]
    return dot(c["forward"][:, :64], special.astype(BF16)).astype(BF16)


def maps(lo, hi, f32, offset, c, w, o_ref):
    lane = lanes((64, 128))
    zero_slot = lane % 32 == 0
    low = lanes((32, 128)) < 64
    f32 = f32.astype(F32)
    re, im = f32[:64], f32[64:]
    h32 = []
    for k in range(2):
        re_p = pltpu.roll(re, 128 - 4 * (k + 1), 1)
        im_p = pltpu.roll(im, 128 - 4 * (k + 1), 1)
        q = jnp.concatenate([re * re_p + im * im_p, im * re_p - re * im_p], 0).astype(BF16)
        h32.append(dot(c["inverse"][:64], q))

    def copy(p):
        return pltpu.make_async_copy(
            w["o"].at[p - lo], o_ref.at[p // 2, p % 2], w["sem"].at[p - lo]
        )

    def correlate(p):
        s, k = p // 2, p % 2
        spectra = []
        for half in range(2):
            columns = []
            for i in (2 * half, 2 * half + 1):
                here = w["f"][s - offset, i].astype(F32)
                there = w["f"][s + k + 1 - offset, i].astype(F32)
                f_re, f_im, p_re, p_im = here[:64], here[64:], there[:64], there[64:]
                q = jnp.concatenate([f_re * p_re + f_im * p_im, f_im * p_re - f_re * p_im], 0)
                columns.append(q.astype(BF16))
            spectra.append(dot(c["inverse"], jnp.concatenate(columns, 1)))
        return spectra

    def last(p, spectra):
        s, k = p // 2, p % 2
        even, odd = [], []
        for i in range(4):
            h = spectra[i // 2][:, 128 * (i % 2) : 128 * (i % 2) + 128]
            special = pltpu.roll(h32[k], (128 - 4 * s - i) % 128, 1)
            h_im = jnp.where(zero_slot, special, h[64:])
            h_cat = jnp.concatenate([h[:64], h_im], 1).astype(BF16)
            even.append(h_cat[:32])
            odd.append(h_cat[32:])
        even = dot(jnp.concatenate(even, 0), c["even"])
        odd = dot(jnp.concatenate(odd, 0), c["odd"])
        return even, odd

    def store(p, even, odd):
        s, k = p // 2, p % 2
        mix = w["mix"].at[p % 2]
        for i in range(4):
            for half in range(2):
                e_scale, o_scale = [
                    w["scale"][n, half, i, s : s + 1] * w["scale"][n, half, i, s + k + 1 : s + k + 2]
                    for n in range(2)
                ]
                e = even[32 * i : 32 * i + 32, 128 * half : 128 * half + 128] * e_scale
                o = odd[32 * i : 32 * i + 32, 128 * half : 128 * half + 128] * o_scale
                mix[i, pl.ds(2 * half, 32, stride=4), :] = jnp.where(low, e, o)
                mix[i, pl.ds(2 * half + 1, 32, stride=4), :] = pltpu.roll(jnp.where(low, o, e), 64, 1)
            w["o"][p - lo, i] = mix[i, :128].astype(BF16)
        copy(p).start()

    ready = {}
    for p in range(lo, hi + 2):
        if p < hi:
            ready[p] = correlate(p)
        if p >= lo + 2:
            store(p - 2, *last(p - 2, ready.pop(p - 2)))
    for p in range(lo, hi):
        copy(p).wait()


SCRATCH = dict(
    g=lambda n: pltpu.VMEM((n, 160, 256), F32),
    mu=lambda n: pltpu.VMEM((5, 8, 256), F32),
    sq=lambda n: pltpu.VMEM((5, 8, 256), F32),
    scale=lambda n: pltpu.VMEM((2, 2, 4, 8, 128), F32),
    mix=lambda n: pltpu.VMEM((2, 4, 136, 128), F32),
)


def own_kernel(xb_ref, xa_ref, ya_ref, yb_ref, s_ref, t_ref, o_ref, f_ref, f32_ref, scale_ref, *scratch):
    c = Tables(t_ref)
    w = dict(zip((*SCRATCH, "o", "sem"), scratch))
    w["f"] = f_ref
    top, bottom = low_high(ya_ref[...], yb_ref[...], "gy")
    sections = [jnp.concatenate([top[s], s_ref[s], bottom[s]], 0) for s in range(6)]
    edges = side_tiles(xa_ref, xb_ref)
    f32 = spectra(0, 0, sections, edges, c, w)
    scale = scales(0, sections, edges, c, w)
    store_scales(scale, w)
    f32_ref[...] = f32
    scale_ref[...] = scale
    maps(0, 9, f32, 0, c, w, o_ref)


def rest_kernel(z_ref, h_ref, f_ref, f32_ref, scale_ref, t_ref, _, o_ref, *scratch):
    c = Tables(t_ref)
    w = dict(zip((*SCRATCH, "f", "o", "sem"), scratch))
    flag = jnp.where(lax.axis_index("gz") == 0, 1.0, 0.0)
    w["f"][0] = f_ref[4]
    w["f"][1] = f_ref[5]
    sections = [z_ref[0], z_ref[1]]
    sides = h_ref[...]
    lower = pltpu.roll(sides.astype(F32), 96, 1).astype(BF16)
    edges = [jnp.concatenate([sides, lower], 0)]
    extra = spectra(6, 2, sections, edges, c, w)
    scale = scales(6, sections, edges, c, w) * flag
    scale = jnp.where(lax.broadcasted_iota(jnp.int32, (32, 256), 0) % 8 >= 6, scale, scale_ref[...])
    store_scales(scale, w)
    f32 = jnp.where(lanes((128, 128)) % 32 >= 24, extra.astype(F32), f32_ref[...].astype(F32))
    maps(9, 12, f32, 4, c, w, o_ref)


def exchange(value_a, value_b, axis):
    sizes = [lax.axis_size(name) for name in AXES]
    along, across = AXES.index(axis), 1 - AXES.index(axis)

    def partner(place, first):
        place = list(place)
        up = place[along] % 2 == first
        moved = place[along] + (1 if up else -1)
        if 0 <= moved < sizes[along]:
            place[along] = moved
        else:
            place[across] ^= 1
        return place

    def pairs(first):
        return [
            (int(np.ravel_multi_index(at, sizes)), int(np.ravel_multi_index(partner(at, first), sizes)))
            for at in np.ndindex(*sizes)
        ]

    value_b = lax.ppermute(value_b, AXES, pairs(1))
    return lax.ppermute(value_a, AXES, pairs(0)), value_b


def other(value):
    return lax.ppermute(value, "gz", [(0, 1), (1, 0)])


def shaped(*shape):
    return jax.ShapeDtypeStruct(shape, BF16)


def params(mib):
    return pltpu.CompilerParams(vmem_limit_bytes=mib * 2**20)


def compute(sections, xa, xb, ya, yb, z, sides, table):
    scratch = [make(6) for make in SCRATCH.values()]
    out, f, f32, scale = pl.pallas_call(
        own_kernel,
        out_shape=(
            shaped(6, 2, 4, 128, 128),
            shaped(6, 4, 128, 128),
            shaped(128, 128),
            jax.ShapeDtypeStruct((32, 256), F32),
        ),
        in_specs=[VMEM] * 6,
        out_specs=(HBM, VMEM, VMEM, VMEM),
        scratch_shapes=scratch + [pltpu.VMEM((9, 4, 128, 128), BF16), pltpu.SemaphoreType.DMA((9,))],
        compiler_params=params(16),
        cost_estimate=pl.CostEstimate(flops=10**9, bytes_accessed=4 * 10**6, transcendentals=0),
    )(xb, xa, ya, yb, sections, table)
    scratch = [make(2) for make in SCRATCH.values()]
    return pl.pallas_call(
        rest_kernel,
        out_shape=shaped(6, 2, 4, 128, 128),
        in_specs=[VMEM] * 6 + [HBM],
        out_specs=HBM,
        scratch_shapes=scratch
        + [
            pltpu.VMEM((4, 4, 128, 128), BF16),
            pltpu.VMEM((3, 4, 128, 128), BF16),
            pltpu.SemaphoreType.DMA((3,)),
        ],
        input_output_aliases={6: 0},
        compiler_params=params(16),
    )(z, sides, f, f32, scale, table, out)


def local(sections):
    pixels = pltpu.with_memory_space_constraint(sections, pltpu.HBM)
    table = constants()[0]
    rows, side, middle = shaped(6, 16, 128), shaped(160, 128), shaped(128, 128)
    ya, yb = pl.pallas_call(
        first_kernel,
        out_shape=(rows, rows),
        in_specs=[HBM],
        out_specs=(VMEM, VMEM),
        scratch_shapes=[pltpu.SemaphoreType.DMA((2,))],
        compiler_params=params(8),
    )(pixels)
    ya, yb = exchange(ya, yb, "gy")
    sections, table, left, right = pl.pallas_call(
        stage_kernel,
        out_shape=(shaped(*sections.shape), shaped(*table.shape), middle, middle),
        in_specs=[HBM, HBM],
        out_specs=(VMEM,) * 4,
        scratch_shapes=[pltpu.SemaphoreType.DMA((2,))],
        compiler_params=params(8),
        cost_estimate=pl.CostEstimate(flops=0, bytes_accessed=2 * 10**6, transcendentals=0),
    )(pixels, pltpu.with_memory_space_constraint(table, pltpu.HBM))
    xa, xb, z = pl.pallas_call(
        sides_kernel,
        out_shape=(side, side, shaped(2, 160, 128)),
        in_specs=[VMEM] * 6,
        out_specs=(VMEM,) * 3,
        compiler_params=params(8),
    )(ya, yb, sections, left, right, table)
    xa, xb = exchange(xa, xb, "gx")
    z = other(z)
    sides = pl.pallas_call(
        halo_kernel,
        out_shape=shaped(80, 128),
        in_specs=[VMEM] * 2,
        out_specs=VMEM,
        compiler_params=params(8),
    )(xb, xa)
    sides = other(sides)
    out = compute(sections, xa, xb, ya, yb, z, sides, table)
    out = out.reshape(6, 2, 4, 32, 4, 128).transpose(0, 1, 2, 4, 3, 5)
    return out.reshape(6, 2, 4, 4, 4096)


def solution(mesh):
    return jax.shard_map(
        local,
        mesh=mesh,
        in_specs=(P("gz", "gy", "gx"),),
        out_specs=P("gz", None, "gy", "gx", None),
        check_vma=False,
    )
```

```python
import functools
import math

import jax
import jax.numpy as jnp
import ml_dtypes
import numpy as np
from jax import lax
from jax.experimental import pallas as pl
from jax.experimental.pallas import tpu as pltpu
from jax.sharding import PartitionSpec as P

PATCH = 64
AXES = ("gx", "gy", "gz")
F32 = jnp.float32
BF16 = jnp.bfloat16
VMEM = pl.BlockSpec(memory_space=pltpu.VMEM)
HBM = pl.BlockSpec(memory_space=pltpu.HBM)


def rounded(values):
    return values.astype(np.float32).astype(ml_dtypes.bfloat16)


@functools.cache
def constants():
    index = np.arange(PATCH)
    angle = (index[:, None] * index[None, :] % PATCH) * (2.0 * math.pi / PATCH)
    cos = rounded(np.cos(angle)).astype(np.float64)
    sin = rounded(np.sin(angle)).astype(np.float64)
    sign = 1.0 - 2.0 * (index % 2)

    rows = np.zeros((160, 2, 4, 32))
    for j in range(4):
        rows[32 * j : 32 * j + 64, 0, j] = cos[:, :32]
        rows[32 * j : 32 * j + 64, 1, j] = -sin[:, :32]
        rows[32 * j : 32 * j + 64, 1, j, 0] = sign
    rows = rows.reshape(160, 256)

    forward = np.block([[cos, sin], [-sin, cos]])
    order = np.concatenate([index[0::2], index[1::2]])
    inverse = np.block([[cos[order], -sin[order]], [sin[order], cos[order]]])

    last = np.zeros((2, 4, 32, 4, 64))
    weight = np.where(index[:32] == 0, 1.0, 2.0)[:, None] / 4096.0
    for j in range(4):
        last[0, j, :, j] = weight * cos[:32]
        last[1, j, :, j] = -weight * sin[:32]
        last[1, j, 0, j] = sign / 4096.0
    even = last.reshape(256, 256)
    odd = last[:, :, :, [1, 0, 3, 2]].reshape(256, 256)

    column = np.full(256, -1000)
    column[:128] = np.arange(128) + 16
    column[128:144] = np.arange(16)
    column[192:208] = np.arange(16) + 144
    inside = np.stack([(column >= 32 * j) & (column < 32 * j + 64) for j in range(4)], 1)
    inside = inside.astype(np.float64)
    same_even = inside[:, [0, 2]] @ inside[:, [0, 2]].T
    same_odd = inside[:, [1, 3]] @ inside[:, [1, 3]].T
    spread = np.repeat(inside, 64, axis=1)
    lane_odd = (np.arange(256) // 64 % 2).astype(np.float64)
    means = np.concatenate([same_even, same_odd], 1)
    totals = np.concatenate([spread * (1 - lane_odd), spread * lane_odd], 0)
    tables = dict(
        own=rows[16:144],
        sides=np.concatenate([rows[:16], rows[144:]], 0),
        forward=forward,
        inverse=inverse,
        even=even,
        odd=odd,
        means=means,
        totals=totals,
    )
    pieces, places, at = [], {}, 0
    for name, table in tables.items():
        height, width = table.shape
        places[name] = (at, height, width // 128)
        pieces += np.split(table, width // 128, 1)
        at += height * width // 128
    return rounded(np.concatenate(pieces, 0)), places


class Tables:
    def __init__(self, ref):
        self.ref = ref

    def __getitem__(self, name):
        at, height, width = constants()[1][name]
        pieces = [self.ref[at + height * n : at + height * (n + 1)] for n in range(width)]
        return jnp.concatenate(pieces, 1) if width > 1 else pieces[0]


def dot(a, b):
    return jnp.dot(a, b, preferred_element_type=F32)


def dot_exact(a, ones):
    high = a.astype(BF16)
    rest = a - high.astype(F32)
    middle = rest.astype(BF16)
    low = (rest - middle.astype(F32)).astype(BF16)
    n = a.shape[0]
    parts = dot(jnp.concatenate([high, middle, low], 0), ones)
    return parts[2 * n :] + parts[n : 2 * n] + parts[:n]


def lanes(shape):
    return lax.broadcasted_iota(jnp.int32, shape, len(shape) - 1)


def first_kernel(s_hbm, a_ref, b_ref, sem):
    odd = lax.axis_index("gy") % 2 == 1
    copies = []
    for n, (out, at) in enumerate(((a_ref, jnp.where(odd, 0, 112)), (b_ref, jnp.where(odd, 112, 0)))):
        rows = s_hbm.at[:, pl.ds(pl.multiple_of(at, 16), 16), :]
        copies.append(pltpu.make_async_copy(rows, out, sem.at[n]))
    for copy in copies:
        copy.start()
    for copy in copies:
        copy.wait()


def pack_sides(blocks):
    lane = lanes(blocks[0].shape)
    left = jnp.zeros(lane.shape, F32)
    right = jnp.zeros(lane.shape, F32)
    for s, block in enumerate(blocks):
        block = block.astype(F32)
        left = jnp.where(lane // 16 == (s + 4) % 8, pltpu.roll(block, (16 * s + 64) % 128, 1) if s != 4 else block, left)
        right = jnp.where(lane // 16 == s, pltpu.roll(block, 16 * s + 16, 1), right)
    return left.astype(BF16), right.astype(BF16)


def stage_kernel(s_hbm, t_hbm, s_ref, t_ref, l_ref, r_ref, sem):
    sections = pltpu.make_async_copy(s_hbm, s_ref, sem.at[0])
    tables = pltpu.make_async_copy(t_hbm, t_ref, sem.at[1])
    sections.start()
    tables.start()
    sections.wait()
    l_ref[...], r_ref[...] = pack_sides([s_ref[s] for s in range(6)])
    tables.wait()


def sides_kernel(ya_ref, yb_ref, s_ref, l_ref, r_ref, _, a_ref, b_ref, z_ref):
    odd = lax.axis_index("gx") % 2 == 1
    top, bottom = low_high(ya_ref[...], yb_ref[...], "gy")
    left, right = pack_sides([jnp.concatenate([top[s], bottom[s]], 0) for s in range(6)])
    left = jnp.concatenate([left[:16], l_ref[...], left[16:]], 0)
    right = jnp.concatenate([right[:16], r_ref[...], right[16:]], 0)
    a_ref[...] = jnp.where(odd, left, right)
    b_ref[...] = jnp.where(odd, right, left)
    for s in range(2):
        z_ref[s] = jnp.concatenate([top[s], s_ref[s], bottom[s]], 0)


def side_tiles(xa_ref, xb_ref):
    left, right = low_high(xa_ref[...], xb_ref[...], "gx")
    low = lanes((160, 128)) < 64
    return jnp.where(low, left, right), jnp.where(low, right, left)


def halo_kernel(xb_ref, xa_ref, h_ref):
    tile = side_tiles(xa_ref, xb_ref)[0].astype(F32)
    own = lanes((80, 128)) % 64 < 32
    h_ref[...] = jnp.where(own, tile[:80], pltpu.roll(tile[80:], 32, 1)).astype(BF16)


def low_high(a, b, axis):
    at = lax.axis_index(axis)
    odd = at % 2 == 1
    zero = jnp.zeros_like(a)
    low = jnp.where(odd, a, jnp.where(at == 0, zero, b))
    high = jnp.where(odd, jnp.where(at == lax.axis_size(axis) - 1, zero, b), a)
    return low, high


def column_stats(block):
    block = block.astype(F32).reshape(5, 32, 128)
    mean = jnp.sum(block, 1, keepdims=True) * (1.0 / 32)
    centred = block - mean
    return mean[:, 0], jnp.sum(centred * centred, 1)


def scales(first, sections, edges, c, w):
    edge_stats = [column_stats(g) for g in edges]
    w["mu"][...] = jnp.zeros(w["mu"].shape, F32)
    w["sq"][...] = jnp.zeros(w["sq"].shape, F32)
    for s, block in enumerate(sections):
        q, g = s % 4, s // 4
        mean, square = column_stats(block)
        mean_e, square_e = edge_stats[g]
        if s:
            mean_e = pltpu.roll(mean_e, 128 - 16 * q - 64 * g, 1)
            square_e = pltpu.roll(square_e, 128 - 16 * q - 64 * g, 1)
        w["mu"][:, first + s, :128] = mean
        w["mu"][:, first + s, 128:] = mean_e
        w["sq"][:, first + s, :128] = square
        w["sq"][:, first + s, 128:] = square_e
    mu = w["mu"][...]
    sq = w["sq"][...]
    mu0, mu1 = mu[:4].reshape(32, 256), mu[1:].reshape(32, 256)
    sq01 = (sq[:4] + sq[1:]).reshape(32, 256)
    sums = dot_exact(mu0 + mu1, c["means"])
    total = []
    for parity in range(2):
        centre = sums[:, 256 * parity : 256 * parity + 256] * (1.0 / 128)
        d0, d1 = mu0 - centre, mu1 - centre
        total.append(sq01 + 32.0 * (d0 * d0 + d1 * d1))
    variance = dot_exact(jnp.concatenate(total, 1), c["totals"]) * (1.0 / 4096)
    return lax.rsqrt(variance + 1e-05) * (1.0 / PATCH)


def store_scales(scale, w):
    for half in range(2):
        part = scale[:, 128 * half : 128 * half + 128]
        w["scale"][0, half] = part.reshape(4, 8, 128)
        w["scale"][1, half] = pltpu.roll(part, 64, 1).reshape(4, 8, 128)


def spectra(first, sections, edges, c, w):
    lane = lanes((64, 128))
    zero_slot = lane % 32 == 0
    sides = c["sides"]
    rows = []
    for s, block in enumerate(sections):
        q = s % 4
        gap0 = jnp.zeros((16 * q, 256), BF16)
        gap1 = jnp.zeros((48 - 16 * q, 256), BF16)
        one, two = (sides[:16], sides[16:]) if s < 4 else (sides[16:], sides[:16])
        pieces = [c["own"], gap0, one, gap1, gap0, two, gap1]
        table = jnp.concatenate([p for p in pieces if p.shape[0]], 0)
        rows.append(dot(jnp.concatenate([block, edges[s // 4]], 1), table))
    special = jnp.zeros((64, 128), F32)
    for s in range(len(sections)):
        for pair in range(2):
            columns = []
            for i in (2 * pair, 2 * pair + 1):
                re = rows[s][32 * i : 32 * i + 64, :128]
                im = rows[s][32 * i : 32 * i + 64, 128:]
                centre = jnp.sum(re, 0, keepdims=True) * (1.0 / 64)
                re = jnp.where(zero_slot, re - centre, re)
                slot = 4 * (s + first) + i
                special = jnp.where(lane % 32 == slot, pltpu.roll(im, slot, 1) if slot else im, special)
                im = jnp.where(zero_slot, 0.0, im)
                columns.append(jnp.concatenate([re, im], 0).astype(BF16))
            f = dot(c["forward"], jnp.concatenate(columns, 1)).astype(BF16)
            for n, i in enumerate((2 * pair, 2 * pair + 1)):
                w["f"][s, i] = f[:, 128 * n : 128 * n + 128]
    return dot(c["forward"][:, :64], special.astype(BF16)).astype(BF16)


def maps(lo, hi, here32, there32, spectrum, c, w, o_ref):
    lane = lanes((64, 128))
    zero_slot = lane % 32 == 0
    low = lanes((32, 128)) < 64
    here32, there32 = here32.astype(F32), there32.astype(F32)
    re_p, im_p = there32[:64], there32[64:]
    h32 = []
    for k in range(2):
        here = pltpu.roll(here32, 4 * (k + 1), 1)
        re, im = here[:64], here[64:]
        q = jnp.concatenate([re * re_p + im * im_p, im * re_p - re * im_p], 0).astype(BF16)
        h32.append(dot(c["inverse"][:64], q))

    def copy(p):
        return pltpu.make_async_copy(
            w["o"].at[p - lo], o_ref.at[p // 2, p % 2], w["sem"].at[p - lo]
        )

    def correlate(p):
        s, k = p // 2, p % 2
        spectra = []
        for half in range(2):
            columns = []
            for i in (2 * half, 2 * half + 1):
                here = spectrum(s, i).astype(F32)
                there = spectrum(s + k + 1, i).astype(F32)
                f_re, f_im, p_re, p_im = here[:64], here[64:], there[:64], there[64:]
                q = jnp.concatenate([f_re * p_re + f_im * p_im, f_im * p_re - f_re * p_im], 0)
                columns.append(q.astype(BF16))
            spectra.append(dot(c["inverse"], jnp.concatenate(columns, 1)))
        return spectra

    def last(p, spectra):
        s, k = p // 2, p % 2
        even, odd = [], []
        for i in range(4):
            h = spectra[i // 2][:, 128 * (i % 2) : 128 * (i % 2) + 128]
            special = pltpu.roll(h32[k], 128 - 4 * (s + k + 1) - i, 1)
            h_im = jnp.where(zero_slot, special, h[64:])
            h_cat = jnp.concatenate([h[:64], h_im], 1).astype(BF16)
            even.append(h_cat[:32])
            odd.append(h_cat[32:])
        even = dot(jnp.concatenate(even, 0), c["even"])
        odd = dot(jnp.concatenate(odd, 0), c["odd"])
        return even, odd

    def store(p, even, odd):
        s, k = p // 2, p % 2
        mix = w["mix"].at[p % 2]
        for i in range(4):
            for half in range(2):
                e_scale, o_scale = [
                    w["scale"][n, half, i, s : s + 1] * w["scale"][n, half, i, s + k + 1 : s + k + 2]
                    for n in range(2)
                ]
                e = even[32 * i : 32 * i + 32, 128 * half : 128 * half + 128] * e_scale
                o = odd[32 * i : 32 * i + 32, 128 * half : 128 * half + 128] * o_scale
                mix[i, pl.ds(2 * half, 32, stride=4), :] = jnp.where(low, e, o)
                mix[i, pl.ds(2 * half + 1, 32, stride=4), :] = pltpu.roll(jnp.where(low, o, e), 64, 1)
            w["o"][p - lo, i] = mix[i, :128].astype(BF16)
        copy(p).start()

    ready = {}
    for p in range(lo, hi + 2):
        if p < hi:
            ready[p] = correlate(p)
        if p >= lo + 2:
            store(p - 2, *last(p - 2, ready.pop(p - 2)))
    for p in range(lo, hi):
        copy(p).wait()


SCRATCH = dict(
    mu=lambda n: pltpu.VMEM((5, 8, 256), F32),
    sq=lambda n: pltpu.VMEM((5, 8, 256), F32),
    scale=lambda n: pltpu.VMEM((2, 2, 4, 8, 128), F32),
    mix=lambda n: pltpu.VMEM((2, 4, 136, 128), F32),
)


def own_kernel(xb_ref, xa_ref, ya_ref, yb_ref, s_ref, t_ref, o_ref, f_ref, f32_ref, scale_ref, *scratch):
    c = Tables(t_ref)
    w = dict(zip((*SCRATCH, "o", "sem"), scratch))
    w["f"] = f_ref
    top, bottom = low_high(ya_ref[...], yb_ref[...], "gy")
    sections = [jnp.concatenate([top[s], s_ref[s], bottom[s]], 0) for s in range(6)]
    edges = side_tiles(xa_ref, xb_ref)
    f32 = spectra(0, sections, edges, c, w)
    scale = scales(0, sections, edges, c, w)
    store_scales(scale, w)
    f32_ref[...] = f32
    scale_ref[...] = scale
    maps(0, 9, f32, f32, lambda s, i: f_ref[s, i], c, w, o_ref)


def rest_kernel(z_ref, h_ref, f_ref, f32_ref, scale_ref, t_ref, _, o_ref, *scratch):
    c = Tables(t_ref)
    w = dict(zip((*SCRATCH, "f", "o", "sem"), scratch))
    flag = jnp.where(lax.axis_index("gz") == 0, 1.0, 0.0)
    sections = [z_ref[0], z_ref[1]]
    sides = h_ref[...]
    lower = pltpu.roll(sides.astype(F32), 96, 1).astype(BF16)
    edges = [jnp.concatenate([sides, lower], 0)]
    extra = spectra(6, sections, edges, c, w)
    scale = scales(6, sections, edges, c, w) * flag
    scale = jnp.where(lax.broadcasted_iota(jnp.int32, (32, 256), 0) % 8 >= 6, scale, scale_ref[...])
    store_scales(scale, w)
    def spectrum(s, i):
        return f_ref[s, i] if s < 6 else w["f"][s - 6, i]

    maps(9, 12, f32_ref[...], extra, spectrum, c, w, o_ref)


def exchange(value_a, value_b, axis):
    sizes = [lax.axis_size(name) for name in AXES]
    along, across = AXES.index(axis), 1 - AXES.index(axis)

    def partner(place, first):
        place = list(place)
        up = place[along] % 2 == first
        moved = place[along] + (1 if up else -1)
        if 0 <= moved < sizes[along]:
            place[along] = moved
        else:
            place[across] ^= 1
        return place

    def pairs(first):
        return [
            (int(np.ravel_multi_index(at, sizes)), int(np.ravel_multi_index(partner(at, first), sizes)))
            for at in np.ndindex(*sizes)
        ]

    value_b = lax.ppermute(value_b, AXES, pairs(1))
    return lax.ppermute(value_a, AXES, pairs(0)), value_b


def other(value):
    return lax.ppermute(value, "gz", [(0, 1), (1, 0)])


def shaped(*shape):
    return jax.ShapeDtypeStruct(shape, BF16)


def params(mib):
    return pltpu.CompilerParams(vmem_limit_bytes=mib * 2**20)


def compute(sections, xa, xb, ya, yb, z, sides, table):
    scratch = [make(6) for make in SCRATCH.values()]
    out, f, f32, scale = pl.pallas_call(
        own_kernel,
        out_shape=(
            shaped(6, 2, 4, 128, 128),
            shaped(6, 4, 128, 128),
            shaped(128, 128),
            jax.ShapeDtypeStruct((32, 256), F32),
        ),
        in_specs=[VMEM] * 6,
        out_specs=(HBM, VMEM, VMEM, VMEM),
        scratch_shapes=scratch + [pltpu.VMEM((9, 4, 128, 128), BF16), pltpu.SemaphoreType.DMA((9,))],
        compiler_params=params(16),
        cost_estimate=pl.CostEstimate(flops=10**9, bytes_accessed=4 * 10**6, transcendentals=0),
    )(xb, xa, ya, yb, sections, table)
    scratch = [make(2) for make in SCRATCH.values()]
    return pl.pallas_call(
        rest_kernel,
        out_shape=shaped(6, 2, 4, 128, 128),
        in_specs=[VMEM] * 6 + [HBM],
        out_specs=HBM,
        scratch_shapes=scratch
        + [
            pltpu.VMEM((2, 4, 128, 128), BF16),
            pltpu.VMEM((3, 4, 128, 128), BF16),
            pltpu.SemaphoreType.DMA((3,)),
        ],
        input_output_aliases={6: 0},
        compiler_params=params(16),
    )(z, sides, f, f32, scale, table, out)


def local(sections):
    pixels = pltpu.with_memory_space_constraint(sections, pltpu.HBM)
    table = constants()[0]
    rows, side, middle = shaped(6, 16, 128), shaped(160, 128), shaped(128, 128)
    ya, yb = pl.pallas_call(
        first_kernel,
        out_shape=(rows, rows),
        in_specs=[HBM],
        out_specs=(VMEM, VMEM),
        scratch_shapes=[pltpu.SemaphoreType.DMA((2,))],
        compiler_params=params(8),
    )(pixels)
    ya, yb = exchange(ya, yb, "gy")
    sections, table, left, right = pl.pallas_call(
        stage_kernel,
        out_shape=(shaped(*sections.shape), shaped(*table.shape), middle, middle),
        in_specs=[HBM, HBM],
        out_specs=(VMEM,) * 4,
        scratch_shapes=[pltpu.SemaphoreType.DMA((2,))],
        compiler_params=params(8),
        cost_estimate=pl.CostEstimate(flops=0, bytes_accessed=2 * 10**6, transcendentals=0),
    )(pixels, pltpu.with_memory_space_constraint(table, pltpu.HBM))
    xa, xb, z = pl.pallas_call(
        sides_kernel,
        out_shape=(side, side, shaped(2, 160, 128)),
        in_specs=[VMEM] * 6,
        out_specs=(VMEM,) * 3,
        compiler_params=params(8),
    )(ya, yb, sections, left, right, table)
    xa, xb = exchange(xa, xb, "gx")
    z = other(z)
    sides = pl.pallas_call(
        halo_kernel,
        out_shape=shaped(80, 128),
        in_specs=[VMEM] * 2,
        out_specs=VMEM,
        compiler_params=params(8),
    )(xb, xa)
    sides = other(sides)
    out = compute(sections, xa, xb, ya, yb, z, sides, table)
    out = out.reshape(6, 2, 4, 32, 4, 128).transpose(0, 1, 2, 4, 3, 5)
    return out.reshape(6, 2, 4, 4, 4096)


def solution(mesh):
    return jax.shard_map(
        local,
        mesh=mesh,
        in_specs=(P("gz", "gy", "gx"),),
        out_specs=P("gz", None, "gy", "gx", None),
        check_vma=False,
    )
```

```python
import functools
import math

import jax
import jax.numpy as jnp
import ml_dtypes
import numpy as np
from jax import lax
from jax.experimental import pallas as pl
from jax.experimental.pallas import tpu as pltpu
from jax.sharding import PartitionSpec as P

PATCH = 64
AXES = ("gx", "gy", "gz")
F32 = jnp.float32
BF16 = jnp.bfloat16
VMEM = pl.BlockSpec(memory_space=pltpu.VMEM)
HBM = pl.BlockSpec(memory_space=pltpu.HBM)


def rounded(values):
    return values.astype(np.float32).astype(ml_dtypes.bfloat16)


@functools.cache
def constants():
    index = np.arange(PATCH)
    angle = (index[:, None] * index[None, :] % PATCH) * (2.0 * math.pi / PATCH)
    cos = rounded(np.cos(angle)).astype(np.float64)
    sin = rounded(np.sin(angle)).astype(np.float64)
    sign = 1.0 - 2.0 * (index % 2)

    rows = np.zeros((160, 2, 4, 32))
    for j in range(4):
        rows[32 * j : 32 * j + 64, 0, j] = cos[:, :32]
        rows[32 * j : 32 * j + 64, 1, j] = -sin[:, :32]
        rows[32 * j : 32 * j + 64, 1, j, 0] = sign
    rows = rows.reshape(160, 256)

    forward = np.block([[cos, sin], [-sin, cos]])
    order = np.concatenate([index[0::2], index[1::2]])
    inverse = np.block([[cos[order], -sin[order]], [sin[order], cos[order]]])

    last = np.zeros((2, 4, 32, 4, 64))
    weight = np.where(index[:32] == 0, 1.0, 2.0)[:, None] / 4096.0
    for j in range(4):
        last[0, j, :, j] = weight * cos[:32]
        last[1, j, :, j] = -weight * sin[:32]
        last[1, j, 0, j] = sign / 4096.0
    even = last.reshape(256, 256)
    odd = last[:, :, :, [1, 0, 3, 2]].reshape(256, 256)

    column = np.full(256, -1000)
    column[:128] = np.arange(128) + 16
    column[128:144] = np.arange(16)
    column[192:208] = np.arange(16) + 144
    inside = np.stack([(column >= 32 * j) & (column < 32 * j + 64) for j in range(4)], 1)
    inside = inside.astype(np.float64)
    same_even = inside[:, [0, 2]] @ inside[:, [0, 2]].T
    same_odd = inside[:, [1, 3]] @ inside[:, [1, 3]].T
    spread = np.repeat(inside, 64, axis=1)
    lane_odd = (np.arange(256) // 64 % 2).astype(np.float64)
    means = np.concatenate([same_even, same_odd], 1)
    totals = np.concatenate([spread * (1 - lane_odd), spread * lane_odd], 0)
    tables = dict(
        own=rows[16:144],
        sides=np.concatenate([rows[:16], rows[144:]], 0),
        forward=forward,
        inverse=inverse,
        even=even,
        odd=odd,
        means=means,
        totals=totals,
    )
    pieces, places, at = [], {}, 0
    for name, table in tables.items():
        height, width = table.shape
        places[name] = (at, height, width // 128)
        pieces += np.split(table, width // 128, 1)
        at += height * width // 128
    return rounded(np.concatenate(pieces, 0)), places


class Tables:
    def __init__(self, ref):
        self.ref = ref

    def __getitem__(self, name):
        at, height, width = constants()[1][name]
        pieces = [self.ref[at + height * n : at + height * (n + 1)] for n in range(width)]
        return jnp.concatenate(pieces, 1) if width > 1 else pieces[0]


def dot(a, b):
    return jnp.dot(a, b, preferred_element_type=F32)


def dot_exact(a, ones):
    high = a.astype(BF16)
    rest = a - high.astype(F32)
    middle = rest.astype(BF16)
    low = (rest - middle.astype(F32)).astype(BF16)
    n = a.shape[0]
    parts = dot(jnp.concatenate([high, middle, low], 0), ones)
    return parts[2 * n :] + parts[n : 2 * n] + parts[:n]


def lanes(shape):
    return lax.broadcasted_iota(jnp.int32, shape, len(shape) - 1)


def first_kernel(s_hbm, a_ref, b_ref, sem):
    odd = lax.axis_index("gy") % 2 == 1
    copies = []
    for n, (out, at) in enumerate(((a_ref, jnp.where(odd, 0, 112)), (b_ref, jnp.where(odd, 112, 0)))):
        rows = s_hbm.at[:, pl.ds(pl.multiple_of(at, 16), 16), :]
        copies.append(pltpu.make_async_copy(rows, out, sem.at[n]))
    for copy in copies:
        copy.start()
    for copy in copies:
        copy.wait()


def pack_sides(blocks):
    lane = lanes(blocks[0].shape)
    left = jnp.zeros(lane.shape, F32)
    right = jnp.zeros(lane.shape, F32)
    for s, block in enumerate(blocks):
        block = block.astype(F32)
        left = jnp.where(lane // 16 == (s + 4) % 8, pltpu.roll(block, (16 * s + 64) % 128, 1) if s != 4 else block, left)
        right = jnp.where(lane // 16 == s, pltpu.roll(block, 16 * s + 16, 1), right)
    return left.astype(BF16), right.astype(BF16)


def stage_kernel(s_hbm, t_hbm, s_ref, t_ref, l_ref, r_ref, sem):
    sections = pltpu.make_async_copy(s_hbm, s_ref, sem.at[0])
    tables = pltpu.make_async_copy(t_hbm, t_ref, sem.at[1])
    sections.start()
    tables.start()
    sections.wait()
    l_ref[...], r_ref[...] = pack_sides([s_ref[s] for s in range(6)])
    tables.wait()


def sides_kernel(ya_ref, yb_ref, s_ref, l_ref, r_ref, _, a_ref, b_ref):
    odd = lax.axis_index("gx") % 2 == 1
    top, bottom = low_high(ya_ref[...], yb_ref[...], "gy")
    left, right = pack_sides([jnp.concatenate([top[s], bottom[s]], 0) for s in range(6)])
    left = jnp.concatenate([left[:16], l_ref[...], left[16:]], 0)
    right = jnp.concatenate([right[:16], r_ref[...], right[16:]], 0)
    a_ref[...] = jnp.where(odd, left, right)
    b_ref[...] = jnp.where(odd, right, left)


def tall_kernel(ya_ref, yb_ref, s_ref, z_ref):
    top, bottom = low_high(ya_ref[:2], yb_ref[:2], "gy")
    for s in range(2):
        z_ref[s] = jnp.concatenate([top[s], s_ref[s], bottom[s]], 0)


def side_tiles(xa_ref, xb_ref):
    left, right = low_high(xa_ref[...], xb_ref[...], "gx")
    low = lanes((160, 128)) < 64
    return jnp.where(low, left, right), jnp.where(low, right, left)


def halo_kernel(xb_ref, xa_ref, h_ref):
    tile = side_tiles(xa_ref, xb_ref)[0].astype(F32)
    own = lanes((80, 128)) % 64 < 32
    h_ref[...] = jnp.where(own, tile[:80], pltpu.roll(tile[80:], 32, 1)).astype(BF16)


def low_high(a, b, axis):
    at = lax.axis_index(axis)
    odd = at % 2 == 1
    zero = jnp.zeros_like(a)
    low = jnp.where(odd, a, jnp.where(at == 0, zero, b))
    high = jnp.where(odd, jnp.where(at == lax.axis_size(axis) - 1, zero, b), a)
    return low, high


def column_stats(block):
    block = block.astype(F32).reshape(5, 32, 128)
    mean = jnp.sum(block, 1, keepdims=True) * (1.0 / 32)
    centred = block - mean
    return mean[:, 0], jnp.sum(centred * centred, 1)


def scales(first, sections, edges, c, w):
    edge_stats = [column_stats(g) for g in edges]
    w["mu"][...] = jnp.zeros(w["mu"].shape, F32)
    w["sq"][...] = jnp.zeros(w["sq"].shape, F32)
    for s, block in enumerate(sections):
        q, g = s % 4, s // 4
        mean, square = column_stats(block)
        mean_e, square_e = edge_stats[g]
        if s:
            mean_e = pltpu.roll(mean_e, 128 - 16 * q - 64 * g, 1)
            square_e = pltpu.roll(square_e, 128 - 16 * q - 64 * g, 1)
        w["mu"][:, first + s, :128] = mean
        w["mu"][:, first + s, 128:] = mean_e
        w["sq"][:, first + s, :128] = square
        w["sq"][:, first + s, 128:] = square_e
    mu = w["mu"][...]
    sq = w["sq"][...]
    mu0, mu1 = mu[:4].reshape(32, 256), mu[1:].reshape(32, 256)
    sq01 = (sq[:4] + sq[1:]).reshape(32, 256)
    sums = dot_exact(mu0 + mu1, c["means"])
    total = []
    for parity in range(2):
        centre = sums[:, 256 * parity : 256 * parity + 256] * (1.0 / 128)
        d0, d1 = mu0 - centre, mu1 - centre
        total.append(sq01 + 32.0 * (d0 * d0 + d1 * d1))
    variance = dot_exact(jnp.concatenate(total, 1), c["totals"]) * (1.0 / 4096)
    return lax.rsqrt(variance + 1e-05) * (1.0 / PATCH)


def store_scales(scale, w):
    for half in range(2):
        part = scale[:, 128 * half : 128 * half + 128]
        w["scale"][0, half] = part.reshape(4, 8, 128)
        w["scale"][1, half] = pltpu.roll(part, 64, 1).reshape(4, 8, 128)


def spectra(first, sections, edges, c, w):
    lane = lanes((64, 128))
    zero_slot = lane % 32 == 0
    sides = c["sides"]
    rows = []
    for s, block in enumerate(sections):
        q = s % 4
        gap0 = jnp.zeros((16 * q, 256), BF16)
        gap1 = jnp.zeros((48 - 16 * q, 256), BF16)
        one, two = (sides[:16], sides[16:]) if s < 4 else (sides[16:], sides[:16])
        pieces = [c["own"], gap0, one, gap1, gap0, two, gap1]
        table = jnp.concatenate([p for p in pieces if p.shape[0]], 0)
        rows.append(dot(jnp.concatenate([block, edges[s // 4]], 1), table))
    special = jnp.zeros((64, 128), F32)
    for s in range(len(sections)):
        for pair in range(2):
            columns = []
            for i in (2 * pair, 2 * pair + 1):
                re = rows[s][32 * i : 32 * i + 64, :128]
                im = rows[s][32 * i : 32 * i + 64, 128:]
                centre = jnp.sum(re, 0, keepdims=True) * (1.0 / 64)
                re = jnp.where(zero_slot, re - centre, re)
                slot = 4 * (s + first) + i
                special = jnp.where(lane % 32 == slot, pltpu.roll(im, slot, 1) if slot else im, special)
                im = jnp.where(zero_slot, 0.0, im)
                columns.append(jnp.concatenate([re, im], 0).astype(BF16))
            f = dot(c["forward"], jnp.concatenate(columns, 1)).astype(BF16)
            for n, i in enumerate((2 * pair, 2 * pair + 1)):
                w["f"][s, i] = f[:, 128 * n : 128 * n + 128]
    return dot(c["forward"][:, :64], special.astype(BF16)).astype(BF16)


def maps(lo, hi, here32, there32, spectrum, c, w, o_ref):
    lane = lanes((64, 128))
    zero_slot = lane % 32 == 0
    low = lanes((32, 128)) < 64
    here32, there32 = here32.astype(F32), there32.astype(F32)
    re_p, im_p = there32[:64], there32[64:]
    h32 = []
    for k in range(2):
        here = pltpu.roll(here32, 4 * (k + 1), 1)
        re, im = here[:64], here[64:]
        q = jnp.concatenate([re * re_p + im * im_p, im * re_p - re * im_p], 0).astype(BF16)
        h32.append(dot(c["inverse"][:64], q))

    def copy(p):
        return pltpu.make_async_copy(
            w["o"].at[p - lo], o_ref.at[p // 2, p % 2], w["sem"].at[p - lo]
        )

    def correlate(p):
        s, k = p // 2, p % 2
        spectra = []
        for half in range(2):
            columns = []
            for i in (2 * half, 2 * half + 1):
                here = spectrum(s, i).astype(F32)
                there = spectrum(s + k + 1, i).astype(F32)
                f_re, f_im, p_re, p_im = here[:64], here[64:], there[:64], there[64:]
                q = jnp.concatenate([f_re * p_re + f_im * p_im, f_im * p_re - f_re * p_im], 0)
                columns.append(q.astype(BF16))
            spectra.append(dot(c["inverse"], jnp.concatenate(columns, 1)))
        return spectra

    def last(p, spectra):
        s, k = p // 2, p % 2
        even, odd = [], []
        for i in range(4):
            h = spectra[i // 2][:, 128 * (i % 2) : 128 * (i % 2) + 128]
            special = pltpu.roll(h32[k], 128 - 4 * (s + k + 1) - i, 1)
            h_im = jnp.where(zero_slot, special, h[64:])
            h_cat = jnp.concatenate([h[:64], h_im], 1).astype(BF16)
            even.append(h_cat[:32])
            odd.append(h_cat[32:])
        even = dot(jnp.concatenate(even, 0), c["even"])
        odd = dot(jnp.concatenate(odd, 0), c["odd"])
        return even, odd

    def store(p, even, odd):
        s, k = p // 2, p % 2
        mix = w["mix"].at[p % 2]
        for i in range(4):
            for half in range(2):
                e_scale, o_scale = [
                    w["scale"][n, half, i, s : s + 1] * w["scale"][n, half, i, s + k + 1 : s + k + 2]
                    for n in range(2)
                ]
                e = even[32 * i : 32 * i + 32, 128 * half : 128 * half + 128] * e_scale
                o = odd[32 * i : 32 * i + 32, 128 * half : 128 * half + 128] * o_scale
                mix[i, pl.ds(2 * half, 32, stride=4), :] = jnp.where(low, e, o)
                mix[i, pl.ds(2 * half + 1, 32, stride=4), :] = pltpu.roll(jnp.where(low, o, e), 64, 1)
            w["o"][p - lo, i] = mix[i, :128].astype(BF16)
        copy(p).start()

    ready = {}
    for p in range(lo, hi + 2):
        if p < hi:
            ready[p] = correlate(p)
        if p >= lo + 2:
            store(p - 2, *last(p - 2, ready.pop(p - 2)))
    for p in range(lo, hi):
        copy(p).wait()


SCRATCH = dict(
    mu=lambda n: pltpu.VMEM((5, 8, 256), F32),
    sq=lambda n: pltpu.VMEM((5, 8, 256), F32),
    scale=lambda n: pltpu.VMEM((2, 2, 4, 8, 128), F32),
    mix=lambda n: pltpu.VMEM((2, 4, 136, 128), F32),
)


def own_kernel(xb_ref, xa_ref, ya_ref, yb_ref, s_ref, t_ref, o_ref, f_ref, f32_ref, scale_ref, *scratch):
    c = Tables(t_ref)
    w = dict(zip((*SCRATCH, "o", "sem"), scratch))
    w["f"] = f_ref
    top, bottom = low_high(ya_ref[...], yb_ref[...], "gy")
    sections = [jnp.concatenate([top[s], s_ref[s], bottom[s]], 0) for s in range(6)]
    edges = side_tiles(xa_ref, xb_ref)
    f32 = spectra(0, sections, edges, c, w)
    scale = scales(0, sections, edges, c, w)
    store_scales(scale, w)
    f32_ref[...] = f32
    scale_ref[...] = scale
    maps(0, 9, f32, f32, lambda s, i: f_ref[s, i], c, w, o_ref)


def rest_kernel(z_ref, h_ref, f_ref, f32_ref, scale_ref, t_ref, _, o_ref, *scratch):
    c = Tables(t_ref)
    w = dict(zip((*SCRATCH, "f", "o", "sem"), scratch))
    flag = jnp.where(lax.axis_index("gz") == 0, 1.0, 0.0)
    sections = [z_ref[0], z_ref[1]]
    sides = h_ref[...]
    lower = pltpu.roll(sides.astype(F32), 96, 1).astype(BF16)
    edges = [jnp.concatenate([sides, lower], 0)]
    extra = spectra(6, sections, edges, c, w)
    scale = scales(6, sections, edges, c, w) * flag
    scale = jnp.where(lax.broadcasted_iota(jnp.int32, (32, 256), 0) % 8 >= 6, scale, scale_ref[...])
    store_scales(scale, w)
    def spectrum(s, i):
        return f_ref[s, i] if s < 6 else w["f"][s - 6, i]

    maps(9, 12, f32_ref[...], extra, spectrum, c, w, o_ref)


def exchange(value_a, value_b, axis):
    sizes = [lax.axis_size(name) for name in AXES]
    along, across = AXES.index(axis), 1 - AXES.index(axis)

    def partner(place, first):
        place = list(place)
        up = place[along] % 2 == first
        moved = place[along] + (1 if up else -1)
        if 0 <= moved < sizes[along]:
            place[along] = moved
        else:
            place[across] ^= 1
        return place

    def pairs(first):
        return [
            (int(np.ravel_multi_index(at, sizes)), int(np.ravel_multi_index(partner(at, first), sizes)))
            for at in np.ndindex(*sizes)
        ]

    value_b = lax.ppermute(value_b, AXES, pairs(1))
    return lax.ppermute(value_a, AXES, pairs(0)), value_b


def other(value):
    return lax.ppermute(value, "gz", [(0, 1), (1, 0)])


def shaped(*shape):
    return jax.ShapeDtypeStruct(shape, BF16)


def params(mib):
    return pltpu.CompilerParams(vmem_limit_bytes=mib * 2**20)


def compute(sections, xa, xb, ya, yb, z, sides, table):
    scratch = [make(6) for make in SCRATCH.values()]
    out, f, f32, scale = pl.pallas_call(
        own_kernel,
        out_shape=(
            shaped(6, 2, 4, 128, 128),
            shaped(6, 4, 128, 128),
            shaped(128, 128),
            jax.ShapeDtypeStruct((32, 256), F32),
        ),
        in_specs=[VMEM] * 6,
        out_specs=(HBM, VMEM, VMEM, VMEM),
        scratch_shapes=scratch + [pltpu.VMEM((9, 4, 128, 128), BF16), pltpu.SemaphoreType.DMA((9,))],
        compiler_params=params(16),
        cost_estimate=pl.CostEstimate(flops=10**9, bytes_accessed=4 * 10**6, transcendentals=0),
    )(xb, xa, ya, yb, sections, table)
    scratch = [make(2) for make in SCRATCH.values()]
    return pl.pallas_call(
        rest_kernel,
        out_shape=shaped(6, 2, 4, 128, 128),
        in_specs=[VMEM] * 6 + [HBM],
        out_specs=HBM,
        scratch_shapes=scratch
        + [
            pltpu.VMEM((2, 4, 128, 128), BF16),
            pltpu.VMEM((3, 4, 128, 128), BF16),
            pltpu.SemaphoreType.DMA((3,)),
        ],
        input_output_aliases={6: 0},
        compiler_params=params(16),
    )(z, sides, f, f32, scale, table, out)


def local(sections):
    pixels = pltpu.with_memory_space_constraint(sections, pltpu.HBM)
    table = constants()[0]
    rows, side, middle = shaped(6, 16, 128), shaped(160, 128), shaped(128, 128)
    ya, yb = pl.pallas_call(
        first_kernel,
        out_shape=(rows, rows),
        in_specs=[HBM],
        out_specs=(VMEM, VMEM),
        scratch_shapes=[pltpu.SemaphoreType.DMA((2,))],
        compiler_params=params(8),
    )(pixels)
    ya, yb = exchange(ya, yb, "gy")
    sections, table, left, right = pl.pallas_call(
        stage_kernel,
        out_shape=(shaped(*sections.shape), shaped(*table.shape), middle, middle),
        in_specs=[HBM, HBM],
        out_specs=(VMEM,) * 4,
        scratch_shapes=[pltpu.SemaphoreType.DMA((2,))],
        compiler_params=params(8),
        cost_estimate=pl.CostEstimate(flops=0, bytes_accessed=2 * 10**6, transcendentals=0),
    )(pixels, pltpu.with_memory_space_constraint(table, pltpu.HBM))
    xa, xb = pl.pallas_call(
        sides_kernel,
        out_shape=(side, side),
        in_specs=[VMEM] * 6,
        out_specs=(VMEM,) * 2,
        compiler_params=params(8),
    )(ya, yb, sections, left, right, table)
    xa, xb = exchange(xa, xb, "gx")
    z = other(
        pl.pallas_call(
            tall_kernel,
            out_shape=shaped(2, 160, 128),
            in_specs=[VMEM] * 3,
            out_specs=VMEM,
            compiler_params=params(8),
        )(ya, yb, sections)
    )
    sides = pl.pallas_call(
        halo_kernel,
        out_shape=shaped(80, 128),
        in_specs=[VMEM] * 2,
        out_specs=VMEM,
        compiler_params=params(8),
    )(xb, xa)
    sides = other(sides)
    out = compute(sections, xa, xb, ya, yb, z, sides, table)
    out = out.reshape(6, 2, 4, 32, 4, 128).transpose(0, 1, 2, 4, 3, 5)
    return out.reshape(6, 2, 4, 4, 4096)


def solution(mesh):
    return jax.shard_map(
        local,
        mesh=mesh,
        in_specs=(P("gz", "gy", "gx"),),
        out_specs=P("gz", None, "gy", "gx", None),
        check_vma=False,
    )
```
